32 devices in a mesh: groups: 2 (over y), tp: 16 (over z, x, core).
Axes of the slice: x: 2, y: 2, z: 4, core: 2. Of those that a mesh axis runs over, the one named last changes fastest.
Arguments:
- stream: bfloat16 [128, 8192], P('groups', 'tp'), parts along dimension 0, may hold values from -6 to 6
- table_rows: bfloat16 [1024, 8192], P('groups', 'tp'), parts along dimension 0, may hold values from -6 to 6
- token_ids: int32 [1, 128], P(None, 'groups'), parts along dimension 1, may hold values from 0 to 511
- norm_gain: float32 [8192], replicated, may hold values from 0.1 to 1.9
- gate_weight: bfloat16 [16, 1024, 13312], P('tp'), may hold values from -0.0625 to 0.0625
- up_weight: bfloat16 [16, 1024, 13312], P('tp'), may hold values from -0.0625 to 0.0625
- down_weight: bfloat16 [16, 13312, 1024], P('tp'), may hold values from -0.0546875 to 0.0546875
Outputs:
- states: bfloat16 [1, 128, 8192], P(None, 'groups', 'tp'), parts along dimension 1
The draws below stay inside these ranges and needn't reach their ends.
There are 2 independent parts, one for each index of `groups`. The reference program is written for one: setup_inputs(seed, part) draws one part's arguments, and reference() takes and returns one part's arrays. A program takes and returns all parts, laid end to end along the dimension named above; an argument that names none is the same for every part. Nothing has to cross between parts.
All inputs are finite; a program needn't handle non-finite values.
Results may differ from the reference program's by a relative error of at most 0.006.
Values may be sent and summed in bfloat16 or wider, within the bound.
No kernel may reach another device: no remote copies, remote signals or barrier semaphores. Data moves between devices by JAX's collectives and lax.ppermute only.
A program may use at most 256 MiB of HBM per device.

```python
import jax
import jax.numpy as jnp
from jax import lax

D = 8192
FF = 26624
BATCH = 64
STEPS = 1
TABLE = 512
D_WAYS = 8
D_BLOCK = 1024
F_BLOCK = 13312
N_TP = 16


def place_ends(entries, key, low, high):
    dims = entries.shape
    place = [jax.random.randint(jax.random.fold_in(key, axis), (), 0, dims[axis]) for axis in range(len(dims))]
    entries = entries.at[tuple(place)].set(low)
    longest = dims.index(max(dims))
    place[longest] = (place[longest] + 1) % dims[longest]
    return entries.at[tuple(place)].set(high)


def raised(values, rng, source, target, shards_of, factor):
    def block_of(position):
        return (jnp.arange(values.shape[position]) // (values.shape[position] // shards_of)).reshape((-1,) + (1,) * (values.ndim - 1 - position))

    near = jax.random.permutation(rng, shards_of)[block_of(target)]
    far = (block_of(target) + shards_of // 2) % shards_of
    return jnp.where((block_of(source) == near) | (block_of(source) == far), factor * values, values)


def level_of(key, shape, shards, smallest, largest):
    def one(axis_at, parts):
        steps = jax.random.uniform(jax.random.fold_in(jax.random.fold_in(key, 6), axis_at), (parts,), jnp.float32, smallest / len(shards), largest / len(shards))
        return jnp.repeat(jnp.exp(steps), shape[axis_at] // parts).reshape((-1,) + (1,) * (len(shape) - axis_at - 1))

    level = one(*shards[0])
    for cut in shards[1:]:
        level = level * one(*cut)
    return level


def noise(own_key, dims, width, reach, pieces=(), kind=jnp.bfloat16):
    result = width * jax.random.normal(own_key, dims, jnp.float32)
    if pieces:
        result = result * level_of(own_key, dims, pieces, -0.22, 0.18)
    return jnp.clip(result, -reach, reach).astype(kind)


def bell_draw_with(key, shape, scale, bound, pieces, heavy, held_as=jnp.bfloat16):
    result = scale * jax.random.normal(key, shape, jnp.float32)
    if pieces:
        result = result * level_of(key, shape, pieces, -0.22, 0.18)
    return jnp.clip(raised(result, jax.random.fold_in(key, 3), *heavy), -bound, bound).astype(held_as)


def setup_inputs(seed: int = 0, part: int = 0) -> dict:
    seeds = jax.random.split(jax.random.key(seed), 8)
    own_keys = jax.random.split(jax.random.fold_in(seeds[7], part), 8)
    return {
        "stream": noise(own_keys[0], (BATCH, D), 1.0, 6.0, ((1, 16),)),
        "table_rows": noise(own_keys[1], (TABLE, D), 1.0, 6.0, ((1, 16),)),
        "token_ids": place_ends(jax.random.randint(own_keys[2], (STEPS, BATCH), 0, TABLE), jax.random.fold_in(own_keys[2], 1), 0, TABLE - 1).astype(jnp.int32),
        "norm_gain": jnp.clip(1.0 + 0.18 * jax.random.normal(seeds[3], (D,), jnp.float32), 0.1, 1.9),
        "gate_weight": noise(seeds[4], (N_TP, D_BLOCK, F_BLOCK), D ** -0.5, 0.0625, ((0, 16),)),
        "up_weight": noise(seeds[5], (N_TP, D_BLOCK, F_BLOCK), D ** -0.5, 0.0625, ((0, 16),)),
        "down_weight": bell_draw_with(seeds[6], (N_TP, F_BLOCK, D_BLOCK), FF ** -0.5, 0.0546875, ((0, 16),), (0, 2, 16, 2.0)),
    }


def full_gate(tiles):
    shaped = tiles.reshape(D_WAYS, N_TP // D_WAYS, D // D_WAYS, tiles.shape[2])
    return jnp.transpose(shaped, (0, 2, 1, 3)).reshape(D, FF)

def full_down(tiles):
    shaped = tiles.reshape(D_WAYS, N_TP // D_WAYS, tiles.shape[1], D // D_WAYS)
    return jnp.transpose(shaped, (1, 2, 0, 3)).reshape(FF, D)

def reference(stream, table_rows, token_ids, norm_gain, gate_weight, up_weight, down_weight):
    gate_full = full_gate(gate_weight)
    up_full = full_gate(up_weight)
    down_full = full_down(down_weight)
    current = stream
    results = []
    for step_index in range(STEPS):
        picked = jnp.take(table_rows, token_ids[step_index], axis=0)
        block_in = (current.astype(jnp.float32) + picked.astype(jnp.float32)).astype(jnp.bfloat16)
        wide_in = block_in.astype(jnp.float32)
        scale_rows = jax.lax.rsqrt(lax.optimization_barrier(jnp.mean(wide_in * wide_in, axis=1, keepdims=True)) + 1e-05)
        normed = (wide_in * scale_rows * norm_gain[None, :]).astype(jnp.bfloat16)
        gate_value = jnp.dot(normed, gate_full, preferred_element_type=jnp.float32)
        up_value = jnp.dot(normed, up_full, preferred_element_type=jnp.float32)
        hidden = (jax.nn.silu(gate_value) * up_value).astype(jnp.bfloat16)
        ffn_out = jnp.dot(hidden, down_full, preferred_element_type=jnp.float32)
        current = (wide_in + ffn_out).astype(jnp.bfloat16)
        results.append(current)
    return jnp.stack(results, axis=0)
```

```python
import jax
import jax.numpy as jnp
from jax import lax
from jax.experimental import pallas as pl
from jax.experimental.pallas import tpu as pltpu
from jax.sharding import PartitionSpec as P

D = 8192
D_WAYS = 8
LANES = 128
VMEM_LIMIT = 40 * 2**20


def ring_order(f_ways):
    if f_ways == 2:
        return [0, 2, 4, 6, 7, 5, 3, 1]
    return list(range(D_WAYS))


def from_partner(value, axis, distance):
    mask = 2**distance
    pairs = [(source, source ^ mask) for source in range(lax.axis_size(axis))]
    return lax.ppermute(value, axis, pairs)


def bit_high(index, bit):
    return index // 2**bit % 2 == 1


def gather_block(local_rows, index, low_bits):
    piece = local_rows
    for bit in range(low_bits):
        other = from_partner(piece, "tp", bit)
        piece = jnp.where(
            bit_high(index, bit),
            jnp.concatenate([other, piece], 1),
            jnp.concatenate([piece, other], 1),
        )
    return piece


def halve_columns(values, index, bit):
    width = values.shape[-1] // 2
    lower = values[..., :width]
    upper = values[..., width:]
    high = bit_high(index, bit)
    return (jnp.where(high, upper, lower), jnp.where(high, lower, upper))


def sum_blocks(partial_value, index, low_bits):
    for bit in reversed(range(low_bits)):
        kept, sent = halve_columns(partial_value, index, bit)
        partial_value = kept + from_partner(sent.astype(jnp.bfloat16), "tp", bit).astype(sent.dtype)
    return partial_value


def up_blocks(x, gate_tile, up_tile, blocks, after):
    depth, units = gate_tile.shape
    width = units // D_WAYS
    rows = x.shape[0]
    count = len(blocks)
    if width % LANES:
        tiles = [
            lax.dynamic_slice_in_dim(tile, block * width, width, 1)
            for block in blocks
            for tile in (gate_tile, up_tile)
        ]
        parts = [jnp.dot(x, tile, preferred_element_type=jnp.float32) for tile in tiles]
        return jnp.stack(parts).reshape(count, 2, rows, width)
    cuts = 2
    cut = depth // cuts

    def kernel(ids, x_ref, gate_ref, up_ref, *rest):
        out_ref, tiles, arrived = rest[-3:]
        copies = []
        for j in range(count):
            columns = pl.ds(pl.multiple_of(ids[j] * width, LANES), width)
            for m, tile_ref in enumerate((gate_ref, up_ref)):
                for c in range(cuts):
                    copy = pltpu.make_async_copy(
                        tile_ref.at[pl.ds(c * cut, cut), columns],
                        tiles.at[2 * j + m, pl.ds(c * cut, cut), :],
                        arrived.at[2 * j + m, c],
                    )
                    copy.start()
                    copies.append((j, m, c, copy))
        for j, m, c, copy in copies:
            copy.wait()
            product = jnp.dot(
                x_ref[:, c * cut : (c + 1) * cut],
                tiles[2 * j + m, c * cut : (c + 1) * cut, :],
                preferred_element_type=jnp.float32,
            )
            if c == 0:
                out_ref[j, m] = product
            else:
                out_ref[j, m] += product

    return pl.pallas_call(
        kernel,
        out_shape=jax.ShapeDtypeStruct((count, 2, rows, width), jnp.float32),
        grid_spec=pltpu.PrefetchScalarGridSpec(
            num_scalar_prefetch=1,
            grid=(),
            in_specs=[pl.BlockSpec(memory_space=pltpu.VMEM)]
            + [pl.BlockSpec(memory_space=pl.ANY)] * (2 + len(after)),
            out_specs=pl.BlockSpec(memory_space=pltpu.VMEM),
            scratch_shapes=[
                pltpu.VMEM((2 * count, depth, width), jnp.bfloat16),
                pltpu.SemaphoreType.DMA((2 * count, cuts)),
            ],
        ),
        compiler_params=pltpu.CompilerParams(vmem_limit_bytes=VMEM_LIMIT),
        cost_estimate=pl.CostEstimate(
            flops=4 * count * rows * depth * width,
            bytes_accessed=4 * count * depth * width,
            transcendentals=0,
        ),
        name="up_blocks",
    )(jnp.stack(blocks), x, gate_tile, up_tile, *after)


def down_blocks(total, hidden, down_tile, blocks, after):
    units, width = down_tile.shape
    depth = units // D_WAYS
    rows = total.shape[0]
    count = len(blocks)
    if depth % LANES:
        for block, value in zip(blocks, hidden):
            tile = lax.dynamic_slice_in_dim(down_tile, block * depth, depth, 0)
            total = total + jnp.dot(value, tile, preferred_element_type=jnp.float32)
        return total
    cuts = depth // LANES
    cut = LANES

    def kernel(ids, total_ref, *rest):
        hidden_refs = rest[:count]
        down_ref = rest[count]
        out_ref, tiles, arrived = rest[-3:]
        copies = []
        for j in range(count):
            for c in range(cuts):
                start = pl.multiple_of(ids[j] * depth + c * cut, LANES)
                copy = pltpu.make_async_copy(
                    down_ref.at[pl.ds(start, cut), :],
                    tiles.at[j, pl.ds(c * cut, cut), :],
                    arrived.at[j, c],
                )
                copy.start()
                copies.append((j, c, copy))
        value = total_ref[...]
        for j, c, copy in copies:
            copy.wait()
            value = value + jnp.dot(
                hidden_refs[j][:, c * cut : (c + 1) * cut],
                tiles[j, c * cut : (c + 1) * cut, :],
                preferred_element_type=jnp.float32,
            )
        out_ref[...] = value

    return pl.pallas_call(
        kernel,
        out_shape=jax.ShapeDtypeStruct((rows, width), jnp.float32),
        grid_spec=pltpu.PrefetchScalarGridSpec(
            num_scalar_prefetch=1,
            grid=(),
            in_specs=[pl.BlockSpec(memory_space=pltpu.VMEM)] * (1 + count)
            + [pl.BlockSpec(memory_space=pl.ANY)] * (1 + len(after)),
            out_specs=pl.BlockSpec(memory_space=pltpu.VMEM),
            scratch_shapes=[
                pltpu.VMEM((count, depth, width), jnp.bfloat16),
                pltpu.SemaphoreType.DMA((count, cuts)),
            ],
        ),
        compiler_params=pltpu.CompilerParams(vmem_limit_bytes=VMEM_LIMIT),
        cost_estimate=pl.CostEstimate(
            flops=2 * count * rows * depth * width,
            bytes_accessed=2 * count * depth * width,
            transcendentals=0,
        ),
        name="down_blocks",
    )(jnp.stack(blocks), total, *hidden, down_tile, *after)


def on_device(stream, table_rows, token_ids, norm_gain, gate_weight, up_weight, down_weight):
    f_ways = lax.axis_size("tp") // D_WAYS
    low_bits = f_ways.bit_length() - 1
    index = lax.axis_index("tp")
    block_pos = index // f_ways
    width = gate_weight.shape[1]
    order = ring_order(f_ways)
    place = jnp.array([order.index(d) for d in range(D_WAYS)], jnp.int32)[block_pos]

    def shift(value, step):
        pairs = [
            (order[p] * f_ways + f, order[(p + step) % D_WAYS] * f_ways + f)
            for p in range(D_WAYS)
            for f in range(f_ways)
        ]
        return lax.ppermute(value, "tp", pairs)

    def at(distance):
        return (place + distance + D_WAYS) % D_WAYS

    gate_tile = gate_weight[0]
    up_tile = up_weight[0]
    down_tile = down_weight[0]
    bf16, f32 = jnp.bfloat16, jnp.float32

    gain_block = lax.dynamic_slice_in_dim(norm_gain, block_pos * width, width)
    picked = jnp.take(table_rows, token_ids[0], axis=0)
    block_in = (stream.astype(f32) + picked.astype(f32)).astype(bf16)
    feature_block = gather_block(block_in, index, low_bits).astype(f32)
    scaled = (feature_block * gain_block[None, :]).astype(bf16)
    wide_in = block_in.astype(f32)
    squares = lax.psum(jnp.sum(wide_in * wide_in, axis=1), "tp")

    far = up_blocks(scaled, gate_tile, up_tile, [at(4)], [])
    right, left = far[0, 0].astype(bf16), far[0, 1].astype(bf16)
    for distance in (3, 2, 1, 0):
        blocks = [at(distance), at(-distance)] if distance else [at(0)]
        own = up_blocks(scaled, gate_tile, up_tile, blocks, [right, left])
        right, left = shift(right, 1), shift(left, -1)
        if distance == 3:
            right = jnp.stack([own[0, 0] + right.astype(f32), own[0, 1]]).astype(bf16)
            left = jnp.stack([own[1, 0], own[1, 1] + left.astype(f32)]).astype(bf16)
        elif distance:
            right = (own[0] + right.astype(f32)).astype(bf16)
            left = (own[1] + left.astype(f32)).astype(bf16)
        else:
            pair = own[0] + right.astype(f32) + left.astype(f32)

    scale_rows = lax.rsqrt(squares[:, None] / D + 1e-05)
    pair = pair * scale_rows
    mine = (jax.nn.silu(pair[0]) * pair[1]).astype(bf16)

    half = mine.shape[0] // 2
    total = jnp.zeros((mine.shape[0], width), f32)
    total = down_blocks(total, [mine], down_tile, [at(0)], [])
    right, left = shift(mine, 1), shift(mine, -1)
    for distance in (1, 2):
        next_right, next_left = shift(right, 1), shift(left, -1)
        total = down_blocks(total, [right, left], down_tile, [at(-distance), at(distance)], [])
        right, left = next_right, next_left
    upper, lower = shift(right[:half], 1), shift(left[half:], -1)
    total = down_blocks(total, [right, left], down_tile, [at(-3), at(3)], [])
    far_hidden = jnp.concatenate([upper, lower], 0)
    total = down_blocks(total, [far_hidden], down_tile, [at(4)], [])

    summed = sum_blocks(total, index, low_bits)
    current = (wide_in + summed).astype(bf16)
    return current[None]


def solution(mesh):
    placed = (
        P("groups", "tp"),
        P("groups", "tp"),
        P(None, "groups"),
        P(),
        P("tp", None, None),
        P("tp", None, None),
        P("tp", None, None),
    )
    return jax.shard_map(
        on_device, mesh=mesh, in_specs=placed, out_specs=P(None, "groups", "tp"), check_vma=False
    )
```

```python
import jax
import jax.numpy as jnp
from jax import lax
from jax.experimental import pallas as pl
from jax.experimental.pallas import tpu as pltpu
from jax.sharding import PartitionSpec as P

D = 8192
D_WAYS = 8
LANES = 128
CHUNK = 512
VMEM_LIMIT = 32 * 2**20
BF16 = jnp.bfloat16
F32 = jnp.float32
IN_VMEM = pl.BlockSpec(memory_space=pltpu.VMEM)
IN_PLACE = pl.BlockSpec(memory_space=pl.ANY)


def from_partner(value, axis, distance):
    mask = 2**distance
    pairs = [(source, source ^ mask) for source in range(lax.axis_size(axis))]
    return lax.ppermute(value, axis, pairs)


def bit_high(index, bit):
    return index // 2**bit % 2 == 1


def gather_block(local_rows, index, low_bits):
    piece = local_rows
    for bit in range(low_bits):
        other = from_partner(piece, "tp", bit)
        piece = jnp.where(
            bit_high(index, bit),
            jnp.concatenate([other, piece], 1),
            jnp.concatenate([piece, other], 1),
        )
    return piece


def halve_columns(values, index, bit):
    width = values.shape[-1] // 2
    lower = values[..., :width]
    upper = values[..., width:]
    high = bit_high(index, bit)
    return (jnp.where(high, upper, lower), jnp.where(high, lower, upper))


def sum_blocks(partial_value, index, low_bits):
    for bit in reversed(range(low_bits)):
        kept, sent = halve_columns(partial_value, index, bit)
        partial_value = kept + from_partner(sent.astype(BF16), "tp", bit).astype(sent.dtype)
    return partial_value


def general(stream, table_rows, token_ids, norm_gain, gate_tile, up_tile, down_tile):
    f_ways = lax.axis_size("tp") // D_WAYS
    low_bits = f_ways.bit_length() - 1
    high_bits = D_WAYS.bit_length() - 1
    index = lax.axis_index("tp")
    block_pos = index // f_ways
    width = gate_tile.shape[0]
    gain_block = lax.dynamic_slice_in_dim(norm_gain, block_pos * width, width)
    picked = jnp.take(table_rows, token_ids[0], axis=0)
    block_in = (stream.astype(F32) + picked.astype(F32)).astype(BF16)
    feature_block = gather_block(block_in, index, low_bits).astype(F32)
    total = jnp.sum(feature_block * feature_block, axis=1)
    for level in range(high_bits):
        total = total + from_partner(total, "tp", low_bits + level)
    scale_rows = lax.rsqrt(total[:, None] / D + 1e-05)
    normed = (feature_block * scale_rows * gain_block[None, :]).astype(BF16)
    pair = jnp.stack(
        [
            jnp.dot(normed, gate_tile, preferred_element_type=F32),
            jnp.dot(normed, up_tile, preferred_element_type=F32),
        ],
        axis=0,
    )
    for level in range(high_bits):
        pair = pair + from_partner(pair, "tp", low_bits + level)
    hidden = (jax.nn.silu(pair[0]) * pair[1]).astype(BF16)
    partial_value = jnp.dot(hidden, down_tile, preferred_element_type=F32)
    summed = sum_blocks(partial_value, index, low_bits)
    return (block_in.astype(F32) + summed).astype(BF16)


def chunks_of(size):
    return [(start, min(CHUNK, size - start)) for start in range(0, size, CHUNK)]


def params():
    return pltpu.CompilerParams(vmem_limit_bytes=VMEM_LIMIT)


def add_rows(token_ids, stream, table_rows):
    entries = table_rows.shape[0]

    def kernel(ids_ref, stream_ref, table_ref, out_ref):
        rows = lax.broadcasted_iota(jnp.int32, (entries, ids_ref.shape[1]), 0)
        chosen = jnp.where(rows == ids_ref[...], 1.0, 0.0).astype(BF16)
        picked = lax.dot_general(
            chosen, table_ref[...], (((0,), (0,)), ((), ())), preferred_element_type=F32
        )
        out_ref[...] = (stream_ref[...].astype(F32) + picked).astype(BF16)

    return pl.pallas_call(
        kernel,
        out_shape=jax.ShapeDtypeStruct(stream.shape, BF16),
        in_specs=[IN_VMEM] * 3,
        out_specs=IN_VMEM,
        name="add_rows",
    )(token_ids, stream, table_rows)


def start_up_copies(block, gate_ref, up_ref, tiles, arrived):
    width = gate_ref.shape[1] // D_WAYS
    depth = gate_ref.shape[0]
    copies = []
    for c, (start, size) in enumerate(chunks_of(2 * width)):
        pieces = []
        for m, ref in enumerate((gate_ref, up_ref)):
            low = max(start, m * width)
            high = min(start + size, (m + 1) * width)
            if low < high:
                column = pl.multiple_of(block * width + (low - m * width), LANES)
                pieces.append(
                    pltpu.make_async_copy(
                        ref.at[:, pl.ds(column, high - low)],
                        tiles.at[:, pl.ds(low, high - low)],
                        arrived.at[c, m],
                    )
                )
        for piece in pieces:
            piece.start()
        copies.append((start, size, pieces))
    return copies


def up_products(x, copies, tiles):
    for start, size, pieces in copies:
        for piece in pieces:
            piece.wait()
        yield start, size, jnp.dot(x, tiles[:, start : start + size], preferred_element_type=F32)


def first_up_block(scalars, own, other, gain, gate_tile, up_tile):
    depth, units = gate_tile.shape
    width = units // D_WAYS
    rows, share = own.shape
    count = len(chunks_of(2 * width))

    def kernel(
        scalars, own_ref, other_ref, gain_ref, gate_ref, up_ref, gate_out, up_out, x_ref, squares_ref, tiles, arrived
    ):
        copies = start_up_copies(scalars[0], gate_ref, up_ref, tiles, arrived)
        squares = jnp.zeros((rows, LANES), F32)
        for side, ref in ((scalars[2], own_ref), (1 - scalars[2], other_ref)):
            place = pl.ds(pl.multiple_of(side * share, LANES), share)
            value = ref[...].astype(F32)
            for lane in range(0, share, LANES):
                squares += value[:, lane : lane + LANES] * value[:, lane : lane + LANES]
            x_ref[:, place] = (value * gain_ref[:, place]).astype(BF16)
        squares_ref[...] = squares
        gate_out[:, :LANES] = squares.astype(BF16)
        for start, size, product in up_products(x_ref[...], copies, tiles):
            product = product.astype(BF16)
            split = min(max(width - start, 0), size)
            if split > 0:
                gate_out[:, LANES + start : LANES + start + split] = product[:, :split]
            if split < size:
                up_out[:, start + split - width : start + size - width] = product[:, split:]

    return pl.pallas_call(
        kernel,
        out_shape=[
            jax.ShapeDtypeStruct((rows, LANES + width), BF16),
            jax.ShapeDtypeStruct((rows, width), BF16),
            jax.ShapeDtypeStruct((rows, depth), BF16),
            jax.ShapeDtypeStruct((rows, LANES), F32),
        ],
        grid_spec=pltpu.PrefetchScalarGridSpec(
            num_scalar_prefetch=1,
            grid=(1,),
            in_specs=[
                IN_VMEM,
                IN_VMEM,
                pl.BlockSpec((1, depth), lambda i, scalars: (0, scalars[1])),
                IN_PLACE,
                IN_PLACE,
            ],
            out_specs=[IN_VMEM] * 4,
            scratch_shapes=[
                pltpu.VMEM((depth, 2 * width), BF16),
                pltpu.SemaphoreType.DMA((count, 2)),
            ],
        ),
        compiler_params=params(),
        cost_estimate=pl.CostEstimate(
            flops=4 * rows * depth * width, bytes_accessed=4 * depth * width, transcendentals=0
        ),
        name="first_up_block",
    )(scalars, own, other, gain, gate_tile, up_tile)


def up_blocks(x, squares, gate_tile, up_tile, blocks, after):
    depth, units = gate_tile.shape
    width = units // D_WAYS
    rows = x.shape[0]
    blocks_n = len(blocks)
    count = len(chunks_of(2 * width))

    def kernel(ids, x_ref, squares_ref, gate_ref, up_ref, *rest):
        out_refs = rest[len(after) : len(after) + blocks_n]
        tiles, arrived = rest[-2:]
        copies = [
            start_up_copies(ids[j], gate_ref, up_ref, tiles.at[j], arrived.at[j]) for j in range(blocks_n)
        ]
        for j in range(blocks_n):
            out_refs[j][:, :LANES] = squares_ref[...]
            for start, size, product in up_products(x_ref[...], copies[j], tiles.at[j]):
                out_refs[j][:, LANES + start : LANES + start + size] = product

    return pl.pallas_call(
        kernel,
        out_shape=[jax.ShapeDtypeStruct((rows, LANES + 2 * width), F32)] * blocks_n,
        grid_spec=pltpu.PrefetchScalarGridSpec(
            num_scalar_prefetch=1,
            grid=(),
            in_specs=[IN_VMEM] * 2 + [IN_PLACE] * (2 + len(after)),
            out_specs=[IN_VMEM] * blocks_n,
            scratch_shapes=[
                pltpu.VMEM((blocks_n, depth, 2 * width), BF16),
                pltpu.SemaphoreType.DMA((blocks_n, count, 2)),
            ],
        ),
        compiler_params=params(),
        cost_estimate=pl.CostEstimate(
            flops=4 * blocks_n * rows * depth * width,
            bytes_accessed=4 * blocks_n * depth * width,
            transcendentals=0,
        ),
        name="up_blocks",
    )(jnp.stack(blocks), x, squares, gate_tile, up_tile, *after)


def start_down_copies(block, down_ref, tiles, arrived):
    depth = down_ref.shape[0] // D_WAYS
    copies = []
    for c, (start, size) in enumerate(chunks_of(depth)):
        copy = pltpu.make_async_copy(
            down_ref.at[pl.ds(pl.multiple_of(block * depth + start, LANES), size), :],
            tiles.at[pl.ds(start, size), :],
            arrived.at[c],
        )
        copy.start()
        copies.append((start, size, copy))
    return copies


def down_products(value, hidden_ref, copies, tiles):
    for start, size, copy in copies:
        copy.wait()
        value = value + jnp.dot(
            hidden_ref[:, start : start + size],
            tiles[start : start + size, :],
            preferred_element_type=F32,
        )
    return value


def down_cost(count, rows, depth, width):
    return pl.CostEstimate(
        flops=2 * count * rows * depth * width,
        bytes_accessed=2 * count * depth * width,
        transcendentals=0,
    )


def down_blocks(total, hidden, down_tile, blocks):
    units, width = down_tile.shape
    depth = units // D_WAYS
    rows = hidden[0].shape[0]
    blocks_n = len(blocks)
    totals = [] if total is None else [total]

    def kernel(ids, *rest):
        hidden_refs = rest[len(totals) : len(totals) + blocks_n]
        down_ref, out_ref, tiles, arrived = rest[len(totals) + blocks_n :]
        copies = [start_down_copies(ids[j], down_ref, tiles.at[j], arrived.at[j]) for j in range(blocks_n)]
        value = rest[0][...] if totals else jnp.zeros((rows, width), F32)
        for j in range(blocks_n):
            value = down_products(value, hidden_refs[j], copies[j], tiles.at[j])
        out_ref[...] = value

    return pl.pallas_call(
        kernel,
        out_shape=jax.ShapeDtypeStruct((rows, width), F32),
        grid_spec=pltpu.PrefetchScalarGridSpec(
            num_scalar_prefetch=1,
            grid=(),
            in_specs=[IN_VMEM] * (len(totals) + blocks_n) + [IN_PLACE],
            out_specs=IN_VMEM,
            scratch_shapes=[
                pltpu.VMEM((blocks_n, depth, width), BF16),
                pltpu.SemaphoreType.DMA((blocks_n, len(chunks_of(depth)))),
            ],
        ),
        compiler_params=params(),
        cost_estimate=down_cost(blocks_n, rows, depth, width),
        name="down_blocks",
    )(jnp.stack(blocks), *totals, *hidden, down_tile)


def last_down_block(scalars, total, upper, lower, down_tile):
    units, width = down_tile.shape
    depth = units // D_WAYS
    rows = total.shape[0]
    half = width // 2

    def kernel(scalars, total_ref, upper_ref, lower_ref, down_ref, kept_ref, sent_ref, hidden, tiles, arrived):
        copies = start_down_copies(scalars[0], down_ref, tiles, arrived)
        hidden[: rows // 2] = upper_ref[...]
        hidden[rows // 2 :] = lower_ref[...]
        value = down_products(total_ref[...], hidden, copies, tiles)
        high = scalars[1] == 1
        kept_ref[...] = jnp.where(high, value[:, half:], value[:, :half])
        sent_ref[...] = jnp.where(high, value[:, :half], value[:, half:]).astype(BF16)

    return pl.pallas_call(
        kernel,
        out_shape=[
            jax.ShapeDtypeStruct((rows, half), F32),
            jax.ShapeDtypeStruct((rows, half), BF16),
        ],
        grid_spec=pltpu.PrefetchScalarGridSpec(
            num_scalar_prefetch=1,
            grid=(),
            in_specs=[IN_VMEM] * 3 + [IN_PLACE],
            out_specs=[IN_VMEM] * 2,
            scratch_shapes=[
                pltpu.VMEM((rows, depth), BF16),
                pltpu.VMEM((depth, width), BF16),
                pltpu.SemaphoreType.DMA((len(chunks_of(depth)),)),
            ],
        ),
        compiler_params=params(),
        cost_estimate=down_cost(1, rows, depth, width),
        name="last_down_block",
    )(scalars, total, upper, lower, down_tile)


def ring(stream, table_rows, token_ids, norm_gain, gate_tile, up_tile, down_tile):
    f_ways = lax.axis_size("tp") // D_WAYS
    low_bits = f_ways.bit_length() - 1
    index = lax.axis_index("tp")
    block_pos = index // f_ways
    side = index % f_ways
    width = gate_tile.shape[1] // D_WAYS
    rows = stream.shape[0]
    order = [0, 2, 4, 6, 7, 5, 3, 1]
    place = jnp.where(block_pos % 2 == 0, block_pos // 2, D_WAYS - 1 - block_pos // 2)

    def shift(value, step):
        pairs = [
            (order[p] * f_ways + f, order[(p + step) % D_WAYS] * f_ways + f)
            for p in range(D_WAYS)
            for f in range(f_ways)
        ]
        return lax.ppermute(value, "tp", pairs)

    def at(distance):
        return (place + distance + D_WAYS) % D_WAYS

    own_in = add_rows(token_ids, stream, table_rows)
    other_in = from_partner(own_in, "tp", 0)

    right, left, scaled, squares = first_up_block(
        jnp.stack([at(4), block_pos, side]), own_in, other_in, norm_gain[None], gate_tile, up_tile
    )
    split = LANES + width
    for distance in (3, 2, 1, 0):
        blocks = [at(distance), at(-distance)] if distance else [at(0)]
        own = up_blocks(scaled, squares, gate_tile, up_tile, blocks, [right, left])
        right, left = shift(right, 1), shift(left, -1)
        if distance == 3:
            right = jnp.concatenate([own[0][:, :split] + right.astype(F32), own[0][:, split:]], 1)
            left = jnp.concatenate([own[1][:, :split], own[1][:, split:] + left.astype(F32)], 1)
            right, left = right.astype(BF16), left.astype(BF16)
        elif distance:
            right = (own[0] + right.astype(F32)).astype(BF16)
            left = (own[1] + left.astype(F32)).astype(BF16)
        else:
            both = own[0] + right.astype(F32) + left.astype(F32)

    both, total_squares = both[:, LANES:], jnp.sum(both[:, :LANES], axis=1, keepdims=True)
    both = both * lax.rsqrt(total_squares / D + 1e-05)
    mine = (jax.nn.silu(both[:, :width]) * both[:, width:]).astype(BF16)

    half = rows // 2
    total = None
    right, left = mine, mine
    for distance in (0, 1, 2, 3):
        if distance == 3:
            next_right, next_left = shift(right[:half], 1), shift(left[half:], -1)
        else:
            next_right, next_left = shift(right, 1), shift(left, -1)
        if distance:
            total = down_blocks(total, [right, left], down_tile, [at(-distance), at(distance)])
        else:
            total = down_blocks(None, [mine], down_tile, [at(0)])
        right, left, total = lax.optimization_barrier((next_right, next_left, total))
    kept, sent = last_down_block(jnp.stack([at(4), side]), total, right, left, down_tile)
    summed = kept + from_partner(sent, "tp", 0).astype(F32)
    return (own_in.astype(F32) + summed).astype(BF16)


def on_device(stream, table_rows, token_ids, norm_gain, gate_weight, up_weight, down_weight):
    units = gate_weight.shape[2]
    fits = lax.axis_size("tp") == 2 * D_WAYS and units % (D_WAYS * LANES) == 0
    body = ring if fits else general
    current = body(
        stream, table_rows, token_ids, norm_gain, gate_weight[0], up_weight[0], down_weight[0]
    )
    return current[None]


def solution(mesh):
    placed = (
        P("groups", "tp"),
        P("groups", "tp"),
        P(None, "groups"),
        P(),
        P("tp", None, None),
        P("tp", None, None),
        P("tp", None, None),
    )
    return jax.shard_map(
        on_device, mesh=mesh, in_specs=placed, out_specs=P(None, "groups", "tp"), check_vma=False
    )
```

```python
import jax
import jax.numpy as jnp
from jax import lax
from jax.experimental import pallas as pl
from jax.experimental.pallas import tpu as pltpu
from jax.sharding import PartitionSpec as P

D = 8192
D_WAYS = 8
LANES = 128
DOWN_CHUNK = 896
VMEM_LIMIT = 32 * 2**20
BF16 = jnp.bfloat16
F32 = jnp.float32
IN_VMEM = pl.BlockSpec(memory_space=pltpu.VMEM)
IN_PLACE = pl.BlockSpec(memory_space=pl.ANY)


def from_partner(value, axis, distance):
    mask = 2**distance
    pairs = [(source, source ^ mask) for source in range(lax.axis_size(axis))]
    return lax.ppermute(value, axis, pairs)


def bit_high(index, bit):
    return index // 2**bit % 2 == 1


def gather_block(local_rows, index, low_bits):
    piece = local_rows
    for bit in range(low_bits):
        other = from_partner(piece, "tp", bit)
        piece = jnp.where(
            bit_high(index, bit),
            jnp.concatenate([other, piece], 1),
            jnp.concatenate([piece, other], 1),
        )
    return piece


def halve_columns(values, index, bit):
    width = values.shape[-1] // 2
    lower = values[..., :width]
    upper = values[..., width:]
    high = bit_high(index, bit)
    return (jnp.where(high, upper, lower), jnp.where(high, lower, upper))


def sum_blocks(partial_value, index, low_bits):
    for bit in reversed(range(low_bits)):
        kept, sent = halve_columns(partial_value, index, bit)
        partial_value = kept + from_partner(sent.astype(BF16), "tp", bit).astype(sent.dtype)
    return partial_value


def general(stream, table_rows, token_ids, norm_gain, gate_tile, up_tile, down_tile):
    f_ways = lax.axis_size("tp") // D_WAYS
    low_bits = f_ways.bit_length() - 1
    high_bits = D_WAYS.bit_length() - 1
    index = lax.axis_index("tp")
    block_pos = index // f_ways
    width = gate_tile.shape[0]
    gain_block = lax.dynamic_slice_in_dim(norm_gain, block_pos * width, width)
    picked = jnp.take(table_rows, token_ids[0], axis=0)
    block_in = (stream.astype(F32) + picked.astype(F32)).astype(BF16)
    feature_block = gather_block(block_in, index, low_bits).astype(F32)
    total = jnp.sum(feature_block * feature_block, axis=1)
    for level in range(high_bits):
        total = total + from_partner(total, "tp", low_bits + level)
    scale_rows = lax.rsqrt(total[:, None] / D + 1e-05)
    normed = (feature_block * scale_rows * gain_block[None, :]).astype(BF16)
    pair = jnp.stack(
        [
            jnp.dot(normed, gate_tile, preferred_element_type=F32),
            jnp.dot(normed, up_tile, preferred_element_type=F32),
        ],
        axis=0,
    )
    for level in range(high_bits):
        pair = pair + from_partner(pair, "tp", low_bits + level)
    hidden = (jax.nn.silu(pair[0]) * pair[1]).astype(BF16)
    partial_value = jnp.dot(hidden, down_tile, preferred_element_type=F32)
    summed = sum_blocks(partial_value, index, low_bits)
    return (block_in.astype(F32) + summed).astype(BF16)


def params():
    return pltpu.CompilerParams(vmem_limit_bytes=VMEM_LIMIT)


def position():
    index = lax.axis_index("tp")
    block = lax.shift_right_logical(index, 1)
    half = lax.shift_right_logical(block, 1)
    place = jnp.where((block & 1) == 0, half, D_WAYS - 1 - half)
    return block, index & 1, place


def at(place, distance):
    return (place + distance + D_WAYS) & (D_WAYS - 1)


def add_rows(token_ids, stream, table_rows, gain):
    entries = table_rows.shape[0]
    rows, share = stream.shape

    def kernel(ids_ref, stream_ref, table_ref, gain_ref, out_ref, message_ref, gains, arrived):
        place = pl.multiple_of(lax.axis_index("tp") * share, LANES)
        copy = pltpu.make_async_copy(gain_ref.at[:, pl.ds(place, share)], gains, arrived)
        copy.start()
        row = lax.broadcasted_iota(jnp.int32, (rows, rows), 0)
        column = lax.broadcasted_iota(jnp.int32, (rows, rows), 1)
        across = jnp.broadcast_to(ids_ref[...].astype(F32), (rows, rows))
        ids = jnp.sum(jnp.where(row == column, across, 0.0), axis=1, keepdims=True).astype(jnp.int32)
        entry = lax.broadcasted_iota(jnp.int32, (rows, entries), 1)
        chosen = jnp.where(entry == ids, 1.0, 0.0).astype(BF16)
        picked = jnp.dot(chosen, table_ref[...], preferred_element_type=F32)
        value = (stream_ref[...].astype(F32) + picked).astype(BF16)
        out_ref[...] = value
        value = value.astype(F32)
        squares = jnp.zeros((rows, LANES), F32)
        for lane in range(0, share, LANES):
            squares += value[:, lane : lane + LANES] * value[:, lane : lane + LANES]
        message_ref[:, share:] = squares.astype(BF16)
        copy.wait()
        message_ref[:, :share] = (value * gains[...]).astype(BF16)

    return pl.pallas_call(
        kernel,
        out_shape=[
            jax.ShapeDtypeStruct((rows, share), BF16),
            jax.ShapeDtypeStruct((rows, share + LANES), BF16),
        ],
        in_specs=[IN_VMEM] * 3 + [IN_PLACE],
        out_specs=[IN_VMEM] * 2,
        scratch_shapes=[pltpu.VMEM((1, share), F32), pltpu.SemaphoreType.DMA],
        name="add_rows",
    )(token_ids, stream, table_rows, gain)


def start_up_copies(block, gate_ref, up_ref, tiles, arrived):
    cuts = arrived.shape[1]
    cut = gate_ref.shape[0] // cuts
    width = gate_ref.shape[1] // D_WAYS
    columns = pl.ds(pl.multiple_of(block * width, LANES), width)
    copies = []
    for m, ref in enumerate((gate_ref, up_ref)):
        for c in range(cuts):
            features = slice(c * cut, (c + 1) * cut)
            copy = pltpu.make_async_copy(
                ref.at[pl.ds(c * cut, cut), columns], tiles.at[m, pl.ds(c * cut, cut), :], arrived.at[m, c]
            )
            copy.start()
            copies.append((m, features, copy))
    return copies


def up_products(x_ref, copies, tiles, out_refs):
    for m, features, copy in copies:
        copy.wait()
        product = jnp.dot(x_ref[:, features], tiles[m, features, :], preferred_element_type=F32)
        if features.start == 0:
            out_refs[m][...] = product
        else:
            out_refs[m][...] += product


def up_scratch(count, depth, width):
    cuts = 2
    return [
        pltpu.VMEM((count, 2, depth, width), BF16),
        pltpu.SemaphoreType.DMA((count, 2, cuts)),
    ]


def up_cost(count, rows, depth, width):
    return pl.CostEstimate(
        flops=4 * count * rows * depth * width,
        bytes_accessed=4 * count * depth * width,
        transcendentals=0,
    )


def first_up_block(own, other, gate_tile, up_tile):
    depth, units = gate_tile.shape
    width = units // D_WAYS
    rows = own.shape[0]
    share = own.shape[1] - LANES

    def kernel(own_ref, other_ref, gate_ref, up_ref, gate_out, up_out, x_ref, squares_ref, products, tiles, arrived):
        _, side, place = position()
        copies = start_up_copies(at(place, 4), gate_ref, up_ref, tiles.at[0], arrived.at[0])
        high = side == 1
        own_x, other_x = own_ref[:, :share], other_ref[:, :share]
        x_ref[:, :share] = jnp.where(high, other_x, own_x)
        x_ref[:, share:] = jnp.where(high, own_x, other_x)
        squares = own_ref[:, share:].astype(F32) + other_ref[:, share:].astype(F32)
        squares_ref[...] = squares
        gate_out[:, :LANES] = squares.astype(BF16)
        up_products(x_ref, copies, tiles.at[0], [products.at[0], products.at[1]])
        gate_out[:, LANES:] = products[0].astype(BF16)
        up_out[...] = products[1].astype(BF16)

    return pl.pallas_call(
        kernel,
        out_shape=[
            jax.ShapeDtypeStruct((rows, LANES + width), BF16),
            jax.ShapeDtypeStruct((rows, width), BF16),
            jax.ShapeDtypeStruct((rows, depth), BF16),
            jax.ShapeDtypeStruct((rows, LANES), F32),
        ],
        in_specs=[IN_VMEM] * 2 + [IN_PLACE] * 2,
        out_specs=[IN_VMEM] * 4,
        scratch_shapes=[pltpu.VMEM((2, rows, width), F32)] + up_scratch(1, depth, width),
        compiler_params=params(),
        cost_estimate=up_cost(1, rows, depth, width),
        name="first_up_block",
    )(own, other, gate_tile, up_tile)


def up_blocks(x, squares, gate_tile, up_tile, distances, after):
    depth, units = gate_tile.shape
    width = units // D_WAYS
    rows = x.shape[0]
    count = len(distances)

    def kernel(x_ref, squares_ref, gate_ref, up_ref, *rest):
        out_refs = rest[len(after) : len(after) + count]
        tiles, arrived = rest[-2:]
        _, _, place = position()
        copies = [
            start_up_copies(at(place, distance), gate_ref, up_ref, tiles.at[j], arrived.at[j])
            for j, distance in enumerate(distances)
        ]
        for j, out_ref in enumerate(out_refs):
            out_ref[:, :LANES] = squares_ref[...]
            pair = [out_ref.at[:, pl.ds(LANES, width)], out_ref.at[:, pl.ds(LANES + width, width)]]
            up_products(x_ref, copies[j], tiles.at[j], pair)

    return pl.pallas_call(
        kernel,
        out_shape=[jax.ShapeDtypeStruct((rows, LANES + 2 * width), F32)] * count,
        in_specs=[IN_VMEM] * 2 + [IN_PLACE] * (2 + len(after)),
        out_specs=[IN_VMEM] * count,
        scratch_shapes=up_scratch(count, depth, width),
        compiler_params=params(),
        cost_estimate=up_cost(count, rows, depth, width),
        name="up_blocks",
    )(x, squares, gate_tile, up_tile, *after)


def down_chunks(depth):
    return [(start, min(DOWN_CHUNK, depth - start)) for start in range(0, depth, DOWN_CHUNK)]


def start_down_copies(block, down_ref, tiles, arrived):
    depth = down_ref.shape[0] // D_WAYS
    copies = []
    for c, (start, size) in enumerate(down_chunks(depth)):
        copy = pltpu.make_async_copy(
            down_ref.at[pl.ds(pl.multiple_of(block * depth + start, LANES), size), :],
            tiles.at[pl.ds(start, size), :],
            arrived.at[c],
        )
        copy.start()
        copies.append((start, size, copy))
    return copies


def down_products(value, hidden_ref, copies, tiles):
    for start, size, copy in copies:
        copy.wait()
        value = value + jnp.dot(
            hidden_ref[:, start : start + size],
            tiles[start : start + size, :],
            preferred_element_type=F32,
        )
    return value


def down_cost(count, rows, depth, width):
    return pl.CostEstimate(
        flops=2 * count * rows * depth * width,
        bytes_accessed=2 * count * depth * width,
        transcendentals=0,
    )


def down_blocks(total, hidden, down_tile, distances, fetch=None):
    units, width = down_tile.shape
    depth = units // D_WAYS
    rows = hidden[0].shape[0]
    count = len(distances)
    totals = [] if total is None else [total]
    fetches = 0 if fetch is None else 1

    def kernel(*rest):
        hidden_refs = rest[len(totals) : len(totals) + count]
        down_ref, out_ref, *fetched, tiles, arrived = rest[len(totals) + count :]
        _, _, place = position()
        copies = [
            start_down_copies(at(place, distance), down_ref, tiles.at[j], arrived.at[j])
            for j, distance in enumerate(distances)
        ]
        ahead = [start_down_copies(at(place, fetch), down_ref, ref, arrived.at[count]) for ref in fetched]
        value = rest[0][...] if totals else jnp.zeros((rows, width), F32)
        for j in range(count):
            value = down_products(value, hidden_refs[j], copies[j], tiles.at[j])
        out_ref[...] = value
        for pieces in ahead:
            for _, _, copy in pieces:
                copy.wait()

    return pl.pallas_call(
        kernel,
        out_shape=[jax.ShapeDtypeStruct((rows, width), F32)]
        + [jax.ShapeDtypeStruct((depth, width), BF16)] * fetches,
        in_specs=[IN_VMEM] * (len(totals) + count) + [IN_PLACE],
        out_specs=[IN_VMEM] * (1 + fetches),
        scratch_shapes=[
            pltpu.VMEM((count, depth, width), BF16),
            pltpu.SemaphoreType.DMA((count + fetches, len(down_chunks(depth)))),
        ],
        compiler_params=params(),
        cost_estimate=down_cost(count + fetches, rows, depth, width),
        name="down_blocks",
    )(*totals, *hidden, down_tile)


def last_down_block(total, upper, lower, tile):
    depth, width = tile.shape
    rows = total.shape[0]
    half = width // 2

    def kernel(total_ref, upper_ref, lower_ref, tile_ref, kept_ref, sent_ref, hidden):
        _, side, _ = position()
        hidden[: rows // 2] = upper_ref[...]
        hidden[rows // 2 :] = lower_ref[...]
        value = total_ref[...] + jnp.dot(hidden[...], tile_ref[...], preferred_element_type=F32)
        high = side == 1
        kept_ref[...] = jnp.where(high, value[:, half:], value[:, :half])
        sent_ref[...] = jnp.where(high, value[:, :half], value[:, half:]).astype(BF16)

    return pl.pallas_call(
        kernel,
        out_shape=[
            jax.ShapeDtypeStruct((rows, half), F32),
            jax.ShapeDtypeStruct((rows, half), BF16),
        ],
        in_specs=[IN_VMEM] * 4,
        out_specs=[IN_VMEM] * 2,
        scratch_shapes=[pltpu.VMEM((rows, depth), BF16)],
        compiler_params=params(),
        cost_estimate=down_cost(1, rows, depth, width),
        name="last_down_block",
    )(total, upper, lower, tile)


def ring(stream, table_rows, token_ids, norm_gain, gate_tile, up_tile, down_tile):
    f_ways = lax.axis_size("tp") // D_WAYS
    width = gate_tile.shape[1] // D_WAYS
    rows = stream.shape[0]
    order = [0, 2, 4, 6, 7, 5, 3, 1]

    def shift(value, step):
        pairs = [
            (order[p] * f_ways + f, order[(p + step) % D_WAYS] * f_ways + f)
            for p in range(D_WAYS)
            for f in range(f_ways)
        ]
        return lax.ppermute(value, "tp", pairs)

    block_in, own = add_rows(token_ids, stream, table_rows, norm_gain[None])
    other = from_partner(own, "tp", 0)

    right, left, scaled, squares = first_up_block(own, other, gate_tile, up_tile)
    split = LANES + width
    for distance in (3, 2, 1, 0):
        distances = [distance, -distance] if distance else [0]
        own = up_blocks(scaled, squares, gate_tile, up_tile, distances, [right, left])
        right, left = shift(right, 1), shift(left, -1)
        if distance == 3:
            right = jnp.concatenate([own[0][:, :split] + right.astype(F32), own[0][:, split:]], 1)
            left = jnp.concatenate([own[1][:, :split], own[1][:, split:] + left.astype(F32)], 1)
            right, left = right.astype(BF16), left.astype(BF16)
        elif distance:
            right = (own[0] + right.astype(F32)).astype(BF16)
            left = (own[1] + left.astype(F32)).astype(BF16)
        else:
            both = own[0] + right.astype(F32) + left.astype(F32)

    both, total_squares = both[:, LANES:], jnp.sum(both[:, :LANES], axis=1, keepdims=True)
    both = both * lax.rsqrt(total_squares / D + 1e-05)
    mine = (jax.nn.silu(both[:, :width]) * both[:, width:]).astype(BF16)

    half = rows // 2
    total = None
    right, left = mine, mine
    for distance in (0, 1, 2, 3):
        if distance == 3:
            next_right, next_left = shift(right[:half], 1), shift(left[half:], -1)
        else:
            next_right, next_left = shift(right, 1), shift(left, -1)
        if distance == 3:
            total, far_tile = down_blocks(total, [right, left], down_tile, [-3, 3], fetch=4)
        elif distance:
            (total,) = down_blocks(total, [right, left], down_tile, [-distance, distance])
        else:
            (total,) = down_blocks(None, [mine], down_tile, [0])
        right, left, total = lax.optimization_barrier((next_right, next_left, total))
    kept, sent = last_down_block(total, right, left, far_tile)
    summed = kept + from_partner(sent, "tp", 0).astype(F32)
    return (block_in.astype(F32) + summed).astype(BF16)


def on_device(stream, table_rows, token_ids, norm_gain, gate_weight, up_weight, down_weight):
    units = gate_weight.shape[2]
    fits = lax.axis_size("tp") == 2 * D_WAYS and units % (D_WAYS * LANES) == 0
    body = ring if fits else general
    current = body(
        stream, table_rows, token_ids, norm_gain, gate_weight[0], up_weight[0], down_weight[0]
    )
    return current[None]


def solution(mesh):
    placed = (
        P("groups", "tp"),
        P("groups", "tp"),
        P(None, "groups"),
        P(),
        P("tp", None, None),
        P("tp", None, None),
        P("tp", None, None),
    )
    return jax.shard_map(
        on_device, mesh=mesh, in_specs=placed, out_specs=P(None, "groups", "tp"), check_vma=False
    )
```

```python
import jax
import jax.numpy as jnp
from jax import lax
from jax.experimental import pallas as pl
from jax.experimental.pallas import tpu as pltpu
from jax.sharding import PartitionSpec as P

D = 8192
D_WAYS = 8
LANES = 128
MIB = 2**20
BF16 = jnp.bfloat16
F32 = jnp.float32
IN_VMEM = pl.BlockSpec(memory_space=pltpu.VMEM)
IN_PLACE = pl.BlockSpec(memory_space=pl.ANY)
IN_HBM = pl.BlockSpec(memory_space=pltpu.HBM)


def from_partner(value, axis, distance):
    mask = 2**distance
    pairs = [(source, source ^ mask) for source in range(lax.axis_size(axis))]
    return lax.ppermute(value, axis, pairs)


def bit_high(index, bit):
    return index // 2**bit % 2 == 1


def gather_block(local_rows, index, low_bits):
    piece = local_rows
    for bit in range(low_bits):
        other = from_partner(piece, "tp", bit)
        piece = jnp.where(
            bit_high(index, bit),
            jnp.concatenate([other, piece], 1),
            jnp.concatenate([piece, other], 1),
        )
    return piece


def halve_columns(values, index, bit):
    width = values.shape[-1] // 2
    lower = values[..., :width]
    upper = values[..., width:]
    high = bit_high(index, bit)
    return (jnp.where(high, upper, lower), jnp.where(high, lower, upper))


def sum_blocks(partial_value, index, low_bits):
    for bit in reversed(range(low_bits)):
        kept, sent = halve_columns(partial_value, index, bit)
        partial_value = kept + from_partner(sent.astype(BF16), "tp", bit).astype(sent.dtype)
    return partial_value


def general(stream, table_rows, token_ids, norm_gain, gate_tile, up_tile, down_tile):
    f_ways = lax.axis_size("tp") // D_WAYS
    low_bits = f_ways.bit_length() - 1
    high_bits = D_WAYS.bit_length() - 1
    index = lax.axis_index("tp")
    block_pos = index // f_ways
    width = gate_tile.shape[0]
    gain_block = lax.dynamic_slice_in_dim(norm_gain, block_pos * width, width)
    picked = jnp.take(table_rows, token_ids[0], axis=0)
    block_in = (stream.astype(F32) + picked.astype(F32)).astype(BF16)
    feature_block = gather_block(block_in, index, low_bits).astype(F32)
    total = jnp.sum(feature_block * feature_block, axis=1)
    for level in range(high_bits):
        total = total + from_partner(total, "tp", low_bits + level)
    scale_rows = lax.rsqrt(total[:, None] / D + 1e-05)
    normed = (feature_block * scale_rows * gain_block[None, :]).astype(BF16)
    pair = jnp.stack(
        [
            jnp.dot(normed, gate_tile, preferred_element_type=F32),
            jnp.dot(normed, up_tile, preferred_element_type=F32),
        ],
        axis=0,
    )
    for level in range(high_bits):
        pair = pair + from_partner(pair, "tp", low_bits + level)
    hidden = (jax.nn.silu(pair[0]) * pair[1]).astype(BF16)
    partial_value = jnp.dot(hidden, down_tile, preferred_element_type=F32)
    summed = sum_blocks(partial_value, index, low_bits)
    return (block_in.astype(F32) + summed).astype(BF16)


def params(mib=26):
    return pltpu.CompilerParams(vmem_limit_bytes=mib * MIB)


def position():
    index = lax.axis_index("tp")
    block = lax.shift_right_logical(index, 1)
    half = lax.shift_right_logical(block, 1)
    place = jnp.where((block & 1) == 0, half, D_WAYS - 1 - half)
    return block, index & 1, place


def at(place, distance):
    return (place + distance + D_WAYS) & (D_WAYS - 1)


def fetch_up_block(gate_tile, up_tile, distance):
    depth, units = gate_tile.shape
    width = units // D_WAYS

    def kernel(gate_ref, up_ref, out_ref, arrived):
        _, _, place = position()
        for _, _, copy in start_up_copies(at(place, distance), gate_ref, up_ref, out_ref, arrived):
            copy.wait()

    return pl.pallas_call(
        kernel,
        out_shape=jax.ShapeDtypeStruct((2, depth, width), BF16),
        in_specs=[IN_HBM] * 2,
        out_specs=IN_VMEM,
        scratch_shapes=[pltpu.SemaphoreType.DMA((2, 1))],
        compiler_params=params(),
        name="fetch_up_block",
    )(gate_tile, up_tile)


def add_rows(token_ids, stream, table_rows, gain, after):
    entries = table_rows.shape[0]
    rows, share = stream.shape

    def kernel(ids_ref, stream_ref, table_ref, gain_ref, after_ref, out_ref, message_ref):
        place = pl.multiple_of(lax.axis_index("tp") * share, LANES)
        row = lax.broadcasted_iota(jnp.int32, (rows, rows), 0)
        column = lax.broadcasted_iota(jnp.int32, (rows, rows), 1)
        across = jnp.broadcast_to(ids_ref[...].astype(F32), (rows, rows))
        ids = jnp.sum(jnp.where(row == column, across, 0.0), axis=1, keepdims=True).astype(jnp.int32)
        entry = lax.broadcasted_iota(jnp.int32, (rows, entries), 1)
        chosen = jnp.where(entry == ids, 1.0, 0.0).astype(BF16)
        picked = jnp.dot(chosen, table_ref[...], preferred_element_type=F32)
        value = (stream_ref[...].astype(F32) + picked).astype(BF16)
        out_ref[...] = value
        value = value.astype(F32)
        squares = jnp.zeros((rows, LANES), F32)
        for lane in range(0, share, LANES):
            squares += value[:, lane : lane + LANES] * value[:, lane : lane + LANES]
        message_ref[:, share:] = squares.astype(BF16)
        message_ref[:, :share] = (value * gain_ref[:, pl.ds(place, share)]).astype(BF16)

    return pl.pallas_call(
        kernel,
        out_shape=[
            jax.ShapeDtypeStruct((rows, share), BF16),
            jax.ShapeDtypeStruct((rows, share + LANES), BF16),
        ],
        in_specs=[IN_VMEM] * 4 + [IN_PLACE],
        out_specs=[IN_VMEM] * 2,
        compiler_params=params(),
        name="add_rows",
    )(token_ids, stream, table_rows, gain, after)


def start_up_copies(block, gate_ref, up_ref, tiles, arrived):
    cuts = arrived.shape[1]
    cut = gate_ref.shape[0] // cuts
    width = gate_ref.shape[1] // D_WAYS
    columns = pl.ds(pl.multiple_of(block * width, LANES), width)
    copies = []
    for m, ref in enumerate((gate_ref, up_ref)):
        for c in range(cuts):
            features = slice(c * cut, (c + 1) * cut)
            copy = pltpu.make_async_copy(
                ref.at[pl.ds(c * cut, cut), columns], tiles.at[m, pl.ds(c * cut, cut), :], arrived.at[m, c]
            )
            copy.start()
            copies.append((m, features, copy))
    return copies


def up_products(x_ref, copies, tiles, out_refs):
    for m, features, copy in copies:
        copy.wait()
        product = jnp.dot(x_ref[:, features], tiles[m, features, :], preferred_element_type=F32)
        if features.start == 0:
            out_refs[m][...] = product
        else:
            out_refs[m][...] += product


def up_scratch(count, depth, width):
    cuts = 2
    return [
        pltpu.VMEM((count, 2, depth, width), BF16),
        pltpu.SemaphoreType.DMA((count, 2, cuts)),
    ]


def up_cost(count, rows, depth, width):
    return pl.CostEstimate(
        flops=4 * count * rows * depth * width,
        bytes_accessed=4 * count * depth * width,
        transcendentals=0,
    )


def first_up_block(own, other, tiles):
    _, depth, width = tiles.shape
    rows = own.shape[0]
    share = own.shape[1] - LANES

    def kernel(own_ref, other_ref, tiles_ref, gate_out, up_out, x_ref, squares_ref):
        _, side, _ = position()
        high = side == 1
        own_x, other_x = own_ref[:, :share], other_ref[:, :share]
        x_ref[:, :share] = jnp.where(high, other_x, own_x)
        x_ref[:, share:] = jnp.where(high, own_x, other_x)
        squares = own_ref[:, share:].astype(F32) + other_ref[:, share:].astype(F32)
        squares_ref[...] = squares
        gate_out[:, :LANES] = squares.astype(BF16)
        x = x_ref[...]
        gate_out[:, LANES:] = jnp.dot(x, tiles_ref[0], preferred_element_type=F32).astype(BF16)
        up_out[...] = jnp.dot(x, tiles_ref[1], preferred_element_type=F32).astype(BF16)

    return pl.pallas_call(
        kernel,
        out_shape=[
            jax.ShapeDtypeStruct((rows, LANES + width), BF16),
            jax.ShapeDtypeStruct((rows, width), BF16),
            jax.ShapeDtypeStruct((rows, depth), BF16),
            jax.ShapeDtypeStruct((rows, LANES), F32),
        ],
        in_specs=[IN_VMEM] * 3,
        out_specs=[IN_VMEM] * 4,
        compiler_params=params(),
        cost_estimate=up_cost(1, rows, depth, width),
        name="first_up_block",
    )(own, other, tiles)


def up_blocks(x, squares, gate_tile, up_tile, distances, after, down_tile=None, fetch=()):
    depth, units = gate_tile.shape
    width = units // D_WAYS
    rows = x.shape[0]
    count = len(distances)
    downs = [down_tile] if fetch else []

    def kernel(x_ref, squares_ref, gate_ref, up_ref, *rest):
        rest = rest[len(after) :]
        down_refs, rest = rest[: len(downs)], rest[len(downs) :]
        out_refs, fetched = rest[:count], rest[count : count + len(fetch)]
        tiles, arrived, fetch_arrived = rest[-3:]
        _, _, place = position()
        copies = [
            start_up_copies(at(place, distance), gate_ref, up_ref, tiles.at[j], arrived.at[j])
            for j, distance in enumerate(distances)
        ]
        ahead = start_down_copies(place, fetch, down_refs, fetched, fetch_arrived)
        for j, out_ref in enumerate(out_refs):
            out_ref[:, :LANES] = squares_ref[...]
            pair = [out_ref.at[:, pl.ds(LANES, width)], out_ref.at[:, pl.ds(LANES + width, width)]]
            up_products(x_ref, copies[j], tiles.at[j], pair)
        for copy in ahead:
            copy.wait()

    return pl.pallas_call(
        kernel,
        out_shape=[jax.ShapeDtypeStruct((rows, LANES + 2 * width), F32)] * count
        + [jax.ShapeDtypeStruct(down_tile_shape(down_tile), BF16) for _ in fetch],
        in_specs=[IN_VMEM] * 2 + [IN_HBM] * 2 + [IN_PLACE] * len(after) + [IN_HBM] * len(downs),
        out_specs=[IN_VMEM] * (count + len(fetch)),
        scratch_shapes=up_scratch(count, depth, width) + [pltpu.SemaphoreType.DMA((max(len(fetch), 1),))],
        compiler_params=params(26 if count == 2 else 14),
        cost_estimate=up_cost(count, rows, depth, width),
        name="up_blocks",
    )(x, squares, gate_tile, up_tile, *after, *downs)


def down_tile_shape(down_tile):
    return (down_tile.shape[0] // D_WAYS, down_tile.shape[1])


def start_down_copies(place, distances, down_refs, tiles, arrived):
    copies = []
    for j, distance in enumerate(distances):
        depth = tiles[j].shape[0]
        start = pl.multiple_of(at(place, distance) * depth, LANES)
        copy = pltpu.make_async_copy(down_refs[0].at[pl.ds(start, depth), :], tiles[j], arrived.at[j])
        copy.start()
        copies.append(copy)
    return copies


def down_cost(count, rows, depth, width):
    return pl.CostEstimate(
        flops=2 * count * rows * depth * width,
        bytes_accessed=2 * count * depth * width,
        transcendentals=0,
    )


def down_blocks(total, hidden, tiles, down_tile, fetch, after):
    depth, width = tiles[0].shape
    half = hidden[0][0].shape[0]
    rows = 2 * half
    count = len(hidden)
    totals = [] if total is None else [total]
    downs = [down_tile] if fetch else []

    def kernel(*rest):
        total_refs, rest = rest[: len(totals)], rest[len(totals) :]
        hidden_refs, tile_refs, rest = rest[: 2 * count], rest[2 * count : 3 * count], rest[3 * count :]
        down_refs, rest = rest[: len(downs)], rest[len(downs) + len(after) :]
        out_ref, *fetched, whole, arrived = rest
        _, _, place = position()
        ahead = start_down_copies(place, fetch, down_refs, fetched, arrived)
        value = total_refs[0][...] if totals else jnp.zeros((rows, width), F32)
        for j, tile_ref in enumerate(tile_refs):
            whole[j, :half] = hidden_refs[2 * j][...]
            whole[j, half:] = hidden_refs[2 * j + 1][...]
            value = value + jnp.dot(whole[j], tile_ref[...], preferred_element_type=F32)
        out_ref[...] = value
        for copy in ahead:
            copy.wait()

    return pl.pallas_call(
        kernel,
        out_shape=[jax.ShapeDtypeStruct((rows, width), F32)]
        + [jax.ShapeDtypeStruct((depth, width), BF16)] * len(fetch),
        in_specs=[IN_VMEM] * (len(totals) + 3 * count) + [IN_HBM] * len(downs) + [IN_PLACE] * len(after),
        out_specs=[IN_VMEM] * (1 + len(fetch)),
        scratch_shapes=[
            pltpu.VMEM((count, rows, depth), BF16),
            pltpu.SemaphoreType.DMA((max(len(fetch), 1),)),
        ],
        compiler_params=params(8),
        cost_estimate=down_cost(count + len(fetch), rows, depth, width),
        name="down_blocks",
    )(*totals, *[half for pair in hidden for half in pair], *tiles, *downs, *after)


def last_down_block(total, upper, lower, tile):
    depth, width = tile.shape
    rows = total.shape[0]
    half = width // 2

    def kernel(total_ref, upper_ref, lower_ref, tile_ref, kept_ref, sent_ref, hidden):
        _, side, _ = position()
        hidden[: rows // 2] = upper_ref[...]
        hidden[rows // 2 :] = lower_ref[...]
        value = total_ref[...] + jnp.dot(hidden[...], tile_ref[...], preferred_element_type=F32)
        high = side == 1
        kept_ref[...] = jnp.where(high, value[:, half:], value[:, :half])
        sent_ref[...] = jnp.where(high, value[:, :half], value[:, half:]).astype(BF16)

    return pl.pallas_call(
        kernel,
        out_shape=[
            jax.ShapeDtypeStruct((rows, half), F32),
            jax.ShapeDtypeStruct((rows, half), BF16),
        ],
        in_specs=[IN_VMEM] * 4,
        out_specs=[IN_VMEM] * 2,
        scratch_shapes=[pltpu.VMEM((rows, depth), BF16)],
        compiler_params=params(8),
        cost_estimate=down_cost(1, rows, depth, width),
        name="last_down_block",
    )(total, upper, lower, tile)


def ring(stream, table_rows, token_ids, norm_gain, gate_tile, up_tile, down_tile):
    f_ways = lax.axis_size("tp") // D_WAYS
    width = gate_tile.shape[1] // D_WAYS
    rows = stream.shape[0]
    order = [0, 2, 4, 6, 7, 5, 3, 1]

    def shift(value, step):
        pairs = [
            (order[p] * f_ways + f, order[(p + step) % D_WAYS] * f_ways + f)
            for p in range(D_WAYS)
            for f in range(f_ways)
        ]
        return lax.ppermute(value, "tp", pairs)

    far_tiles = fetch_up_block(gate_tile, up_tile, 4)
    block_in, own = add_rows(token_ids, stream, table_rows, norm_gain[None], far_tiles)
    other = from_partner(own, "tp", 0)

    right, left, scaled, squares = first_up_block(own, other, far_tiles)
    split = LANES + width
    down_tiles = []
    for distance, fetch in ((3, ()), (2, (0, -1)), (1, (1, -2)), (0, (2, -3, 3, 4))):
        distances = [distance, -distance] if distance else [0]
        found = up_blocks(scaled, squares, gate_tile, up_tile, distances, [right, left], down_tile, fetch)
        own = found[: len(distances)]
        down_tiles += found[len(distances) :]
        right, left = shift(right, 1), shift(left, -1)
        if distance == 3:
            right = jnp.concatenate([own[0][:, :split] + right.astype(F32), own[0][:, split:]], 1)
            left = jnp.concatenate([own[1][:, :split], own[1][:, split:] + left.astype(F32)], 1)
            right, left = right.astype(BF16), left.astype(BF16)
        elif distance:
            right = (own[0] + right.astype(F32)).astype(BF16)
            left = (own[1] + left.astype(F32)).astype(BF16)
        else:
            both = own[0] + right.astype(F32) + left.astype(F32)

    both, total_squares = both[:, LANES:], jnp.sum(both[:, :LANES], axis=1, keepdims=True)
    both = both * lax.rsqrt(total_squares / D + 1e-05)
    mine = (jax.nn.silu(both[:, :width]) * both[:, width:]).astype(BF16)

    half = rows // 2
    upper, lower = mine[:half], mine[half:]
    total = None
    hidden = [(upper, lower)]
    upper_right, upper_left, lower_right, lower_left = upper, upper, lower, lower
    for distance, fetch in ((0, ()), (1, ()), (2, ()), (3, ())):
        tiles, down_tiles = down_tiles[: len(hidden)], down_tiles[len(hidden) :]
        upper_right = shift(upper_right, 1)
        lower_left = shift(lower_left, -1)
        if distance < 3:
            upper_left = shift(upper_left, -1)
            lower_right = shift(lower_right, 1)
            after = [upper_right, upper_left]
        else:
            after = []
        total, *fetched = down_blocks(total, hidden, tiles, down_tile, fetch, after)
        down_tiles += fetched
        lower_right, lower_left, total = lax.optimization_barrier((lower_right, lower_left, total))
        hidden = [(upper_right, lower_right), (upper_left, lower_left)]
    (far_tile,) = down_tiles
    kept, sent = last_down_block(total, upper_right, lower_left, far_tile)
    summed = kept + from_partner(sent, "tp", 0).astype(F32)
    return (block_in.astype(F32) + summed).astype(BF16)


def on_device(stream, table_rows, token_ids, norm_gain, gate_weight, up_weight, down_weight):
    units = gate_weight.shape[2]
    fits = lax.axis_size("tp") == 2 * D_WAYS and units % (D_WAYS * LANES) == 0
    body = ring if fits else general
    current = body(
        stream, table_rows, token_ids, norm_gain, gate_weight[0], up_weight[0], down_weight[0]
    )
    return current[None]


def solution(mesh):
    placed = (
        P("groups", "tp"),
        P("groups", "tp"),
        P(None, "groups"),
        P(),
        P("tp", None, None),
        P("tp", None, None),
        P("tp", None, None),
    )
    return jax.shard_map(
        on_device, mesh=mesh, in_specs=placed, out_specs=P(None, "groups", "tp"), check_vma=False
    )
```

```python
import jax
import jax.numpy as jnp
from jax import lax
from jax.experimental import pallas as pl
from jax.experimental.pallas import tpu as pltpu
from jax.sharding import PartitionSpec as P

D = 8192
D_WAYS = 8
LANES = 128
MIB = 2**20
BF16 = jnp.bfloat16
F32 = jnp.float32
IN_VMEM = pl.BlockSpec(memory_space=pltpu.VMEM)
IN_PLACE = pl.BlockSpec(memory_space=pl.ANY)
IN_HBM = pl.BlockSpec(memory_space=pltpu.HBM)


def from_partner(value, axis, distance):
    mask = 2**distance
    pairs = [(source, source ^ mask) for source in range(lax.axis_size(axis))]
    return lax.ppermute(value, axis, pairs)


def bit_high(index, bit):
    return index // 2**bit % 2 == 1


def gather_block(local_rows, index, low_bits):
    piece = local_rows
    for bit in range(low_bits):
        other = from_partner(piece, "tp", bit)
        piece = jnp.where(
            bit_high(index, bit),
            jnp.concatenate([other, piece], 1),
            jnp.concatenate([piece, other], 1),
        )
    return piece


def halve_columns(values, index, bit):
    width = values.shape[-1] // 2
    lower = values[..., :width]
    upper = values[..., width:]
    high = bit_high(index, bit)
    return (jnp.where(high, upper, lower), jnp.where(high, lower, upper))


def sum_blocks(partial_value, index, low_bits):
    for bit in reversed(range(low_bits)):
        kept, sent = halve_columns(partial_value, index, bit)
        partial_value = kept + from_partner(sent.astype(BF16), "tp", bit).astype(sent.dtype)
    return partial_value


def general(stream, table_rows, token_ids, norm_gain, gate_tile, up_tile, down_tile):
    f_ways = lax.axis_size("tp") // D_WAYS
    low_bits = f_ways.bit_length() - 1
    high_bits = D_WAYS.bit_length() - 1
    index = lax.axis_index("tp")
    block_pos = index // f_ways
    width = gate_tile.shape[0]
    gain_block = lax.dynamic_slice_in_dim(norm_gain, block_pos * width, width)
    picked = jnp.take(table_rows, token_ids[0], axis=0)
    block_in = (stream.astype(F32) + picked.astype(F32)).astype(BF16)
    feature_block = gather_block(block_in, index, low_bits).astype(F32)
    total = jnp.sum(feature_block * feature_block, axis=1)
    for level in range(high_bits):
        total = total + from_partner(total, "tp", low_bits + level)
    scale_rows = lax.rsqrt(total[:, None] / D + 1e-05)
    normed = (feature_block * scale_rows * gain_block[None, :]).astype(BF16)
    pair = jnp.stack(
        [
            jnp.dot(normed, gate_tile, preferred_element_type=F32),
            jnp.dot(normed, up_tile, preferred_element_type=F32),
        ],
        axis=0,
    )
    for level in range(high_bits):
        pair = pair + from_partner(pair, "tp", low_bits + level)
    hidden = (jax.nn.silu(pair[0]) * pair[1]).astype(BF16)
    partial_value = jnp.dot(hidden, down_tile, preferred_element_type=F32)
    summed = sum_blocks(partial_value, index, low_bits)
    return (block_in.astype(F32) + summed).astype(BF16)


def params(mib=26):
    return pltpu.CompilerParams(vmem_limit_bytes=mib * MIB)


def position():
    index = lax.axis_index("tp")
    block = lax.shift_right_logical(index, 1)
    half = lax.shift_right_logical(block, 1)
    place = jnp.where((block & 1) == 0, half, D_WAYS - 1 - half)
    return block, index & 1, place


def at(place, distance):
    return (place + distance + D_WAYS) & (D_WAYS - 1)


def fetch_up_block(gate_tile, up_tile, distance):
    depth, units = gate_tile.shape
    width = units // D_WAYS

    def kernel(gate_ref, up_ref, out_ref, arrived):
        _, _, place = position()
        for _, _, copy in start_up_copies(at(place, distance), gate_ref, up_ref, out_ref, arrived):
            copy.wait()

    return pl.pallas_call(
        kernel,
        out_shape=jax.ShapeDtypeStruct((2, depth, width), BF16),
        in_specs=[IN_HBM] * 2,
        out_specs=IN_VMEM,
        scratch_shapes=[pltpu.SemaphoreType.DMA((2, 1))],
        compiler_params=params(),
        name="fetch_up_block",
    )(gate_tile, up_tile)


def add_rows(token_ids, stream, table_rows, gain, after):
    entries = table_rows.shape[0]
    rows, share = stream.shape

    def kernel(ids_ref, stream_ref, table_ref, gain_ref, after_ref, out_ref, message_ref):
        place = pl.multiple_of(lax.axis_index("tp") * share, LANES)
        row = lax.broadcasted_iota(jnp.int32, (rows, rows), 0)
        column = lax.broadcasted_iota(jnp.int32, (rows, rows), 1)
        across = jnp.broadcast_to(ids_ref[...].astype(F32), (rows, rows))
        ids = jnp.sum(jnp.where(row == column, across, 0.0), axis=1, keepdims=True).astype(jnp.int32)
        entry = lax.broadcasted_iota(jnp.int32, (rows, entries), 1)
        chosen = jnp.where(entry == ids, 1.0, 0.0).astype(BF16)
        picked = jnp.dot(chosen, table_ref[...], preferred_element_type=F32)
        value = (stream_ref[...].astype(F32) + picked).astype(BF16)
        out_ref[...] = value
        value = value.astype(F32)
        squares = jnp.zeros((rows, LANES), F32)
        for lane in range(0, share, LANES):
            squares += value[:, lane : lane + LANES] * value[:, lane : lane + LANES]
        message_ref[:, share:] = squares.astype(BF16)
        message_ref[:, :share] = (value * gain_ref[:, pl.ds(place, share)]).astype(BF16)

    return pl.pallas_call(
        kernel,
        out_shape=[
            jax.ShapeDtypeStruct((rows, share), BF16),
            jax.ShapeDtypeStruct((rows, share + LANES), BF16),
        ],
        in_specs=[IN_VMEM] * 4 + [IN_PLACE],
        out_specs=[IN_VMEM] * 2,
        compiler_params=params(),
        name="add_rows",
    )(token_ids, stream, table_rows, gain, after)


def start_up_copies(block, gate_ref, up_ref, tiles, arrived, gate_here=None):
    cuts = arrived.shape[1]
    cut = gate_ref.shape[0] // cuts
    width = gate_ref.shape[1] // D_WAYS
    columns = pl.ds(pl.multiple_of(block * width, LANES), width)
    copies = []
    for m, ref in enumerate((gate_ref, up_ref)):
        for c in range(cuts):
            features = slice(c * cut, (c + 1) * cut)
            copy = pltpu.make_async_copy(
                ref.at[pl.ds(c * cut, cut), columns], tiles.at[m, pl.ds(c * cut, cut), :], arrived.at[m, c]
            )
            if m == 0 and gate_here is not None:
                pl.when(jnp.logical_not(gate_here))(copy.start)
            else:
                copy.start()
            copies.append((m, features, copy))
    return copies


def up_products(x_ref, copies, tiles, out_refs):
    for m, features, copy in copies:
        copy.wait()
        product = jnp.dot(x_ref[:, features], tiles[m, features, :], preferred_element_type=F32)
        if features.start == 0:
            out_refs[m][...] = product
        else:
            out_refs[m][...] += product


def up_products_ahead(x_ref, copies, tiles, out_refs, gate_here, ahead_ref):
    @pl.when(gate_here)
    def _():
        out_refs[0][...] = jnp.dot(x_ref[...], ahead_ref[...], preferred_element_type=F32)

    @pl.when(jnp.logical_not(gate_here))
    def _():
        up_products(x_ref, [copy for copy in copies if copy[0] == 0], tiles, out_refs)

    up_products(x_ref, [copy for copy in copies if copy[0] == 1], tiles, out_refs)


def up_scratch(count, depth, width):
    cuts = 2
    return [
        pltpu.VMEM((count, 2, depth, width), BF16),
        pltpu.SemaphoreType.DMA((count, 2, cuts)),
    ]


def up_cost(count, rows, depth, width):
    return pl.CostEstimate(
        flops=4 * count * rows * depth * width,
        bytes_accessed=4 * count * depth * width,
        transcendentals=0,
    )


def first_up_block(own, other, tiles, gate_tile):
    _, depth, width = tiles.shape
    rows = own.shape[0]
    share = own.shape[1] - LANES

    def kernel(own_ref, other_ref, tiles_ref, gate_ref, gate_out, up_out, x_ref, squares_ref, ahead_ref, arrived):
        _, side, place = position()
        high = side == 1
        columns = pl.ds(pl.multiple_of(at(place, 3) * width, LANES), width)
        copy = pltpu.make_async_copy(gate_ref.at[:, columns], ahead_ref, arrived)

        @pl.when(side == 0)
        def _():
            copy.start()

        own_x, other_x = own_ref[:, :share], other_ref[:, :share]
        x_ref[:, :share] = jnp.where(high, other_x, own_x)
        x_ref[:, share:] = jnp.where(high, own_x, other_x)
        squares = own_ref[:, share:].astype(F32) + other_ref[:, share:].astype(F32)
        squares_ref[...] = squares
        gate_out[:, :LANES] = squares.astype(BF16)
        x = x_ref[...]
        gate_out[:, LANES:] = jnp.dot(x, tiles_ref[0], preferred_element_type=F32).astype(BF16)
        up_out[...] = jnp.dot(x, tiles_ref[1], preferred_element_type=F32).astype(BF16)

        @pl.when(side == 0)
        def _():
            copy.wait()

    return pl.pallas_call(
        kernel,
        out_shape=[
            jax.ShapeDtypeStruct((rows, LANES + width), BF16),
            jax.ShapeDtypeStruct((rows, width), BF16),
            jax.ShapeDtypeStruct((rows, depth), BF16),
            jax.ShapeDtypeStruct((rows, LANES), F32),
            jax.ShapeDtypeStruct((depth, width), BF16),
        ],
        in_specs=[IN_VMEM] * 3 + [IN_HBM],
        out_specs=[IN_VMEM] * 5,
        scratch_shapes=[pltpu.SemaphoreType.DMA],
        compiler_params=params(),
        cost_estimate=up_cost(1, rows, depth, width),
        name="first_up_block",
    )(own, other, tiles, gate_tile)


def up_blocks(x, squares, gate_tile, up_tile, distances, after, down_tile=None, fetch=(), ahead_tile=None):
    depth, units = gate_tile.shape
    width = units // D_WAYS
    rows = x.shape[0]
    count = len(distances)
    downs = [down_tile] if fetch else []
    aheads = [] if ahead_tile is None else [ahead_tile]

    def kernel(x_ref, squares_ref, gate_ref, up_ref, *rest):
        rest = rest[len(after) :]
        down_refs, rest = rest[: len(downs)], rest[len(downs) :]
        ahead_refs, rest = rest[: len(aheads)], rest[len(aheads) :]
        out_refs, fetched = rest[:count], rest[count : count + len(fetch)]
        tiles, arrived, fetch_arrived = rest[-3:]
        _, side, place = position()
        here = side == 0
        copies = [
            start_up_copies(
                at(place, distance),
                gate_ref,
                up_ref,
                tiles.at[j],
                arrived.at[j],
                here if j == 0 and aheads else None,
            )
            for j, distance in enumerate(distances)
        ]
        ahead = start_down_copies(place, fetch, down_refs, fetched, fetch_arrived)
        for j, out_ref in enumerate(out_refs):
            out_ref[:, :LANES] = squares_ref[...]
            pair = [out_ref.at[:, pl.ds(LANES, width)], out_ref.at[:, pl.ds(LANES + width, width)]]
            if j == 0 and aheads:
                up_products_ahead(x_ref, copies[j], tiles.at[j], pair, here, ahead_refs[0])
            else:
                up_products(x_ref, copies[j], tiles.at[j], pair)
        for copy in ahead:
            copy.wait()

    return pl.pallas_call(
        kernel,
        out_shape=[jax.ShapeDtypeStruct((rows, LANES + 2 * width), F32)] * count
        + [jax.ShapeDtypeStruct(down_tile_shape(down_tile), BF16) for _ in fetch],
        in_specs=[IN_VMEM] * 2
        + [IN_HBM] * 2
        + [IN_PLACE] * len(after)
        + [IN_HBM] * len(downs)
        + [IN_VMEM] * len(aheads),
        out_specs=[IN_VMEM] * (count + len(fetch)),
        scratch_shapes=up_scratch(count, depth, width) + [pltpu.SemaphoreType.DMA((max(len(fetch), 1),))],
        compiler_params=params(26 if count == 2 else 14),
        cost_estimate=up_cost(count, rows, depth, width),
        name="up_blocks",
    )(x, squares, gate_tile, up_tile, *after, *downs, *aheads)


def down_tile_shape(down_tile):
    return (down_tile.shape[0] // D_WAYS, down_tile.shape[1])


def start_down_copies(place, distances, down_refs, tiles, arrived):
    copies = []
    for j, distance in enumerate(distances):
        depth = tiles[j].shape[0]
        start = pl.multiple_of(at(place, distance) * depth, LANES)
        copy = pltpu.make_async_copy(down_refs[0].at[pl.ds(start, depth), :], tiles[j], arrived.at[j])
        copy.start()
        copies.append(copy)
    return copies


def down_cost(count, rows, depth, width):
    return pl.CostEstimate(
        flops=2 * count * rows * depth * width,
        bytes_accessed=2 * count * depth * width,
        transcendentals=0,
    )


def down_blocks(total, hidden, tiles, down_tile, fetch, after):
    depth, width = tiles[0].shape
    half = hidden[0][0].shape[0]
    rows = 2 * half
    count = len(hidden)
    totals = [] if total is None else [total]
    downs = [down_tile] if fetch else []

    def kernel(*rest):
        total_refs, rest = rest[: len(totals)], rest[len(totals) :]
        hidden_refs, tile_refs, rest = rest[: 2 * count], rest[2 * count : 3 * count], rest[3 * count :]
        down_refs, rest = rest[: len(downs)], rest[len(downs) + len(after) :]
        out_ref, *fetched, whole, arrived = rest
        _, _, place = position()
        ahead = start_down_copies(place, fetch, down_refs, fetched, arrived)
        value = total_refs[0][...] if totals else jnp.zeros((rows, width), F32)
        for j, tile_ref in enumerate(tile_refs):
            whole[j, :half] = hidden_refs[2 * j][...]
            whole[j, half:] = hidden_refs[2 * j + 1][...]
            value = value + jnp.dot(whole[j], tile_ref[...], preferred_element_type=F32)
        out_ref[...] = value
        for copy in ahead:
            copy.wait()

    return pl.pallas_call(
        kernel,
        out_shape=[jax.ShapeDtypeStruct((rows, width), F32)]
        + [jax.ShapeDtypeStruct((depth, width), BF16)] * len(fetch),
        in_specs=[IN_VMEM] * (len(totals) + 3 * count) + [IN_HBM] * len(downs) + [IN_PLACE] * len(after),
        out_specs=[IN_VMEM] * (1 + len(fetch)),
        scratch_shapes=[
            pltpu.VMEM((count, rows, depth), BF16),
            pltpu.SemaphoreType.DMA((max(len(fetch), 1),)),
        ],
        compiler_params=params(8),
        cost_estimate=down_cost(count + len(fetch), rows, depth, width),
        name="down_blocks",
    )(*totals, *[half for pair in hidden for half in pair], *tiles, *downs, *after)


def last_down_block(total, upper, lower, tile):
    depth, width = tile.shape
    rows = total.shape[0]
    half = width // 2

    def kernel(total_ref, upper_ref, lower_ref, tile_ref, kept_ref, sent_ref, hidden):
        _, side, _ = position()
        hidden[: rows // 2] = upper_ref[...]
        hidden[rows // 2 :] = lower_ref[...]
        value = total_ref[...] + jnp.dot(hidden[...], tile_ref[...], preferred_element_type=F32)
        high = side == 1
        kept_ref[...] = jnp.where(high, value[:, half:], value[:, :half])
        sent_ref[...] = jnp.where(high, value[:, :half], value[:, half:]).astype(BF16)

    return pl.pallas_call(
        kernel,
        out_shape=[
            jax.ShapeDtypeStruct((rows, half), F32),
            jax.ShapeDtypeStruct((rows, half), BF16),
        ],
        in_specs=[IN_VMEM] * 4,
        out_specs=[IN_VMEM] * 2,
        scratch_shapes=[pltpu.VMEM((rows, depth), BF16)],
        compiler_params=params(8),
        cost_estimate=down_cost(1, rows, depth, width),
        name="last_down_block",
    )(total, upper, lower, tile)


def ring(stream, table_rows, token_ids, norm_gain, gate_tile, up_tile, down_tile):
    f_ways = lax.axis_size("tp") // D_WAYS
    width = gate_tile.shape[1] // D_WAYS
    rows = stream.shape[0]
    order = [0, 2, 4, 6, 7, 5, 3, 1]

    def shift(value, step):
        pairs = [
            (order[p] * f_ways + f, order[(p + step) % D_WAYS] * f_ways + f)
            for p in range(D_WAYS)
            for f in range(f_ways)
        ]
        return lax.ppermute(value, "tp", pairs)

    far_tiles = fetch_up_block(gate_tile, up_tile, 4)
    block_in, own = add_rows(token_ids, stream, table_rows, norm_gain[None], far_tiles)
    other = from_partner(own, "tp", 0)

    right, left, scaled, squares, ahead_tile = first_up_block(own, other, far_tiles, gate_tile)
    split = LANES + width
    down_tiles = []
    for distance, fetch in ((3, ()), (2, (0, -1)), (1, (1, -2)), (0, (2, -3, 3, 4))):
        distances = [distance, -distance] if distance else [0]
        ahead = ahead_tile if distance == 3 else None
        found = up_blocks(scaled, squares, gate_tile, up_tile, distances, [right, left], down_tile, fetch, ahead)
        own = found[: len(distances)]
        down_tiles += found[len(distances) :]
        right, left = shift(right, 1), shift(left, -1)
        if distance == 3:
            right = jnp.concatenate([own[0][:, :split] + right.astype(F32), own[0][:, split:]], 1)
            left = jnp.concatenate([own[1][:, :split], own[1][:, split:] + left.astype(F32)], 1)
            right, left = right.astype(BF16), left.astype(BF16)
        elif distance:
            right = (own[0] + right.astype(F32)).astype(BF16)
            left = (own[1] + left.astype(F32)).astype(BF16)
        else:
            both = own[0] + right.astype(F32) + left.astype(F32)

    both, total_squares = both[:, LANES:], jnp.sum(both[:, :LANES], axis=1, keepdims=True)
    both = both * lax.rsqrt(total_squares / D + 1e-05)
    mine = (jax.nn.silu(both[:, :width]) * both[:, width:]).astype(BF16)

    half = rows // 2
    upper, lower = mine[:half], mine[half:]
    total = None
    hidden = [(upper, lower)]
    upper_right, upper_left, lower_right, lower_left = upper, upper, lower, lower
    for distance, fetch in ((0, ()), (1, ()), (2, ()), (3, ())):
        tiles, down_tiles = down_tiles[: len(hidden)], down_tiles[len(hidden) :]
        upper_right = shift(upper_right, 1)
        lower_left = shift(lower_left, -1)
        if distance < 3:
            upper_left = shift(upper_left, -1)
            lower_right = shift(lower_right, 1)
            after = [upper_right, upper_left]
        else:
            after = []
        total, *fetched = down_blocks(total, hidden, tiles, down_tile, fetch, after)
        down_tiles += fetched
        lower_right, lower_left, total = lax.optimization_barrier((lower_right, lower_left, total))
        hidden = [(upper_right, lower_right), (upper_left, lower_left)]
    (far_tile,) = down_tiles
    kept, sent = last_down_block(total, upper_right, lower_left, far_tile)
    summed = kept + from_partner(sent, "tp", 0).astype(F32)
    return (block_in.astype(F32) + summed).astype(BF16)


def on_device(stream, table_rows, token_ids, norm_gain, gate_weight, up_weight, down_weight):
    units = gate_weight.shape[2]
    fits = lax.axis_size("tp") == 2 * D_WAYS and units % (D_WAYS * LANES) == 0
    body = ring if fits else general
    current = body(
        stream, table_rows, token_ids, norm_gain, gate_weight[0], up_weight[0], down_weight[0]
    )
    return current[None]


def solution(mesh):
    placed = (
        P("groups", "tp"),
        P("groups", "tp"),
        P(None, "groups"),
        P(),
        P("tp", None, None),
        P("tp", None, None),
        P("tp", None, None),
    )
    return jax.shard_map(
        on_device, mesh=mesh, in_specs=placed, out_specs=P(None, "groups", "tp"), check_vma=False
    )
```

```python
import jax
import jax.numpy as jnp
from jax import lax
from jax.experimental import pallas as pl
from jax.experimental.pallas import tpu as pltpu
from jax.sharding import PartitionSpec as P

D = 8192
D_WAYS = 8
LANES = 128
MIB = 2**20
BF16 = jnp.bfloat16
F32 = jnp.float32
IN_VMEM = pl.BlockSpec(memory_space=pltpu.VMEM)
IN_PLACE = pl.BlockSpec(memory_space=pl.ANY)
IN_HBM = pl.BlockSpec(memory_space=pltpu.HBM)


def from_partner(value, axis, distance):
    mask = 2**distance
    pairs = [(source, source ^ mask) for source in range(lax.axis_size(axis))]
    return lax.ppermute(value, axis, pairs)


def bit_high(index, bit):
    return index // 2**bit % 2 == 1


def gather_block(local_rows, index, low_bits):
    piece = local_rows
    for bit in range(low_bits):
        other = from_partner(piece, "tp", bit)
        piece = jnp.where(
            bit_high(index, bit),
            jnp.concatenate([other, piece], 1),
            jnp.concatenate([piece, other], 1),
        )
    return piece


def halve_columns(values, index, bit):
    width = values.shape[-1] // 2
    lower = values[..., :width]
    upper = values[..., width:]
    high = bit_high(index, bit)
    return (jnp.where(high, upper, lower), jnp.where(high, lower, upper))


def sum_blocks(partial_value, index, low_bits):
    for bit in reversed(range(low_bits)):
        kept, sent = halve_columns(partial_value, index, bit)
        partial_value = kept + from_partner(sent.astype(BF16), "tp", bit).astype(sent.dtype)
    return partial_value


def general(stream, table_rows, token_ids, norm_gain, gate_tile, up_tile, down_tile):
    f_ways = lax.axis_size("tp") // D_WAYS
    low_bits = f_ways.bit_length() - 1
    high_bits = D_WAYS.bit_length() - 1
    index = lax.axis_index("tp")
    block_pos = index // f_ways
    width = gate_tile.shape[0]
    gain_block = lax.dynamic_slice_in_dim(norm_gain, block_pos * width, width)
    picked = jnp.take(table_rows, token_ids[0], axis=0)
    block_in = (stream.astype(F32) + picked.astype(F32)).astype(BF16)
    feature_block = gather_block(block_in, index, low_bits).astype(F32)
    total = jnp.sum(feature_block * feature_block, axis=1)
    for level in range(high_bits):
        total = total + from_partner(total, "tp", low_bits + level)
    scale_rows = lax.rsqrt(total[:, None] / D + 1e-05)
    normed = (feature_block * scale_rows * gain_block[None, :]).astype(BF16)
    pair = jnp.stack(
        [
            jnp.dot(normed, gate_tile, preferred_element_type=F32),
            jnp.dot(normed, up_tile, preferred_element_type=F32),
        ],
        axis=0,
    )
    for level in range(high_bits):
        pair = pair + from_partner(pair, "tp", low_bits + level)
    hidden = (jax.nn.silu(pair[0]) * pair[1]).astype(BF16)
    partial_value = jnp.dot(hidden, down_tile, preferred_element_type=F32)
    summed = sum_blocks(partial_value, index, low_bits)
    return (block_in.astype(F32) + summed).astype(BF16)


def params(mib=26):
    return pltpu.CompilerParams(vmem_limit_bytes=mib * MIB)


def position():
    index = lax.axis_index("tp")
    block = lax.shift_right_logical(index, 1)
    half = lax.shift_right_logical(block, 1)
    place = jnp.where((block & 1) == 0, half, D_WAYS - 1 - half)
    return block, index & 1, place


def at(place, distance):
    return (place + distance + D_WAYS) & (D_WAYS - 1)


def fetch_up_block(gate_tile, up_tile, distance):
    depth, units = gate_tile.shape
    width = units // D_WAYS

    def kernel(gate_ref, up_ref, out_ref, arrived):
        _, _, place = position()
        for _, _, copy in start_up_copies(at(place, distance), gate_ref, up_ref, out_ref, arrived):
            copy.wait()

    return pl.pallas_call(
        kernel,
        out_shape=jax.ShapeDtypeStruct((2, depth, width), BF16),
        in_specs=[IN_HBM] * 2,
        out_specs=IN_VMEM,
        scratch_shapes=[pltpu.SemaphoreType.DMA((2, 1))],
        compiler_params=params(),
        name="fetch_up_block",
    )(gate_tile, up_tile)


def add_rows(token_ids, stream, table_rows, gain, after):
    entries = table_rows.shape[0]
    rows, share = stream.shape

    def kernel(ids_ref, stream_ref, table_ref, gain_ref, after_ref, out_ref, message_ref):
        place = pl.multiple_of(lax.axis_index("tp") * share, LANES)
        row = lax.broadcasted_iota(jnp.int32, (rows, rows), 0)
        column = lax.broadcasted_iota(jnp.int32, (rows, rows), 1)
        across = jnp.broadcast_to(ids_ref[...].astype(F32), (rows, rows))
        ids = jnp.sum(jnp.where(row == column, across, 0.0), axis=1, keepdims=True).astype(jnp.int32)
        entry = lax.broadcasted_iota(jnp.int32, (rows, entries), 1)
        chosen = jnp.where(entry == ids, 1.0, 0.0).astype(BF16)
        picked = jnp.dot(chosen, table_ref[...], preferred_element_type=F32)
        value = (stream_ref[...].astype(F32) + picked).astype(BF16)
        out_ref[...] = value
        value = value.astype(F32)
        squares = jnp.zeros((rows, LANES), F32)
        for lane in range(0, share, LANES):
            squares += value[:, lane : lane + LANES] * value[:, lane : lane + LANES]
        message_ref[:, share:] = squares.astype(BF16)
        message_ref[:, :share] = (value * gain_ref[:, pl.ds(place, share)]).astype(BF16)

    return pl.pallas_call(
        kernel,
        out_shape=[
            jax.ShapeDtypeStruct((rows, share), BF16),
            jax.ShapeDtypeStruct((rows, share + LANES), BF16),
        ],
        in_specs=[IN_VMEM] * 4 + [IN_PLACE],
        out_specs=[IN_VMEM] * 2,
        compiler_params=params(),
        name="add_rows",
    )(token_ids, stream, table_rows, gain, after)


def start_up_copies(block, gate_ref, up_ref, tiles, arrived, skipped=None, skip=None):
    cuts = arrived.shape[1]
    cut = gate_ref.shape[0] // cuts
    width = gate_ref.shape[1] // D_WAYS
    columns = pl.ds(pl.multiple_of(block * width, LANES), width)
    copies = []
    for m, ref in enumerate((gate_ref, up_ref)):
        for c in range(cuts):
            features = slice(c * cut, (c + 1) * cut)
            copy = pltpu.make_async_copy(
                ref.at[pl.ds(c * cut, cut), columns], tiles.at[m, pl.ds(c * cut, cut), :], arrived.at[m, c]
            )
            if m == skipped:
                pl.when(jnp.logical_not(skip))(copy.start)
            else:
                copy.start()
            copies.append((m, features, copy))
    return copies


def up_products(x_ref, copies, tiles, out_refs):
    for m, features, copy in copies:
        copy.wait()
        product = jnp.dot(x_ref[:, features], tiles[m, features, :], preferred_element_type=F32)
        if features.start == 0:
            out_refs[m][...] = product
        else:
            out_refs[m][...] += product


def up_products_ahead(x_ref, copies, tiles, out_refs, gate_here, ahead_ref):
    @pl.when(gate_here)
    def _():
        out_refs[0][...] = jnp.dot(x_ref[...], ahead_ref[...], preferred_element_type=F32)

    @pl.when(jnp.logical_not(gate_here))
    def _():
        up_products(x_ref, [copy for copy in copies if copy[0] == 0], tiles, out_refs)

    up_products(x_ref, [copy for copy in copies if copy[0] == 1], tiles, out_refs)


def up_scratch(count, depth, width):
    cuts = 2
    return [
        pltpu.VMEM((count, 2, depth, width), BF16),
        pltpu.SemaphoreType.DMA((count, 2, cuts)),
    ]


def up_cost(count, rows, depth, width):
    return pl.CostEstimate(
        flops=4 * count * rows * depth * width,
        bytes_accessed=4 * count * depth * width,
        transcendentals=0,
    )


def first_up_block(own, other, tiles, gate_tile):
    _, depth, width = tiles.shape
    rows = own.shape[0]
    share = own.shape[1] - LANES

    def kernel(own_ref, other_ref, tiles_ref, gate_ref, gate_out, up_out, x_ref, squares_ref, ahead_ref, arrived):
        _, side, place = position()
        high = side == 1
        columns = pl.ds(pl.multiple_of(at(place, 3) * width, LANES), width)
        copy = pltpu.make_async_copy(gate_ref.at[:, columns], ahead_ref, arrived)

        @pl.when(side == 0)
        def _():
            copy.start()

        own_x, other_x = own_ref[:, :share], other_ref[:, :share]
        x_ref[:, :share] = jnp.where(high, other_x, own_x)
        x_ref[:, share:] = jnp.where(high, own_x, other_x)
        squares = own_ref[:, share:].astype(F32) + other_ref[:, share:].astype(F32)
        squares_ref[...] = squares
        gate_out[:, :LANES] = squares.astype(BF16)
        x = x_ref[...]
        gate_out[:, LANES:] = jnp.dot(x, tiles_ref[0], preferred_element_type=F32).astype(BF16)
        up_out[...] = jnp.dot(x, tiles_ref[1], preferred_element_type=F32).astype(BF16)

        @pl.when(side == 0)
        def _():
            copy.wait()

    return pl.pallas_call(
        kernel,
        out_shape=[
            jax.ShapeDtypeStruct((rows, LANES + width), BF16),
            jax.ShapeDtypeStruct((rows, width), BF16),
            jax.ShapeDtypeStruct((rows, depth), BF16),
            jax.ShapeDtypeStruct((rows, LANES), F32),
            jax.ShapeDtypeStruct((depth, width), BF16),
        ],
        in_specs=[IN_VMEM] * 3 + [IN_HBM],
        out_specs=[IN_VMEM] * 5,
        scratch_shapes=[pltpu.SemaphoreType.DMA],
        compiler_params=params(),
        cost_estimate=up_cost(1, rows, depth, width),
        name="first_up_block",
    )(own, other, tiles, gate_tile)


def up_blocks(x, squares, gate_tile, up_tile, distances, after, down_tile=None, fetch=(), ahead_tile=None):
    depth, units = gate_tile.shape
    width = units // D_WAYS
    rows = x.shape[0]
    count = len(distances)
    downs = [down_tile] if fetch else []
    aheads = [] if ahead_tile is None else [ahead_tile]

    def kernel(x_ref, squares_ref, gate_ref, up_ref, *rest):
        rest = rest[len(after) :]
        down_refs, rest = rest[: len(downs)], rest[len(downs) :]
        ahead_refs, rest = rest[: len(aheads)], rest[len(aheads) :]
        out_refs, fetched = rest[:count], rest[count : count + len(fetch)]
        tiles, arrived, fetch_arrived = rest[-3:]
        _, side, place = position()
        here = side == 0
        copies = [
            start_up_copies(
                at(place, distance),
                gate_ref,
                up_ref,
                tiles.at[j],
                arrived.at[j],
                0 if j == 0 and aheads else None,
                here,
            )
            for j, distance in enumerate(distances)
        ]
        ahead = start_down_copies(place, fetch, down_refs, fetched, fetch_arrived)
        for j, out_ref in enumerate(out_refs):
            out_ref[:, :LANES] = squares_ref[...]
            pair = [out_ref.at[:, pl.ds(LANES, width)], out_ref.at[:, pl.ds(LANES + width, width)]]
            if j == 0 and aheads:
                up_products_ahead(x_ref, copies[j], tiles.at[j], pair, here, ahead_refs[0])
            else:
                up_products(x_ref, copies[j], tiles.at[j], pair)
        for copy in ahead:
            copy.wait()

    return pl.pallas_call(
        kernel,
        out_shape=[jax.ShapeDtypeStruct((rows, LANES + 2 * width), F32)] * count
        + [jax.ShapeDtypeStruct(down_tile_shape(down_tile), BF16) for _ in fetch],
        in_specs=[IN_VMEM] * 2
        + [IN_HBM] * 2
        + [IN_PLACE] * len(after)
        + [IN_HBM] * len(downs)
        + [IN_VMEM] * len(aheads),
        out_specs=[IN_VMEM] * (count + len(fetch)),
        scratch_shapes=up_scratch(count, depth, width) + [pltpu.SemaphoreType.DMA((max(len(fetch), 1),))],
        compiler_params=params(26 if count == 2 else 14),
        cost_estimate=up_cost(count, rows, depth, width),
        name="up_blocks",
    )(x, squares, gate_tile, up_tile, *after, *downs, *aheads)


def own_block(x, gate_tile, up_tile, after, down_tile, fetch):
    depth, units = gate_tile.shape
    width = units // D_WAYS
    rows = x.shape[0]

    def kernel(x_ref, gate_ref, up_ref, *rest):
        down_ref, tiles, gate_out, up_out, *fetched, arrived, fetch_arrived = rest[len(after) :]
        _, side, place = position()
        copies = start_up_copies(at(place, 0), gate_ref, up_ref, tiles, arrived)
        ahead = start_down_copies(place, fetch, [down_ref], fetched, fetch_arrived)

        @pl.when(side == 0)
        def _():
            up_products(x_ref, copies, tiles, [gate_out, up_out])

        @pl.when(side == 1)
        def _():
            for _, _, copy in copies:
                copy.wait()

        for copy in ahead:
            copy.wait()

    return pl.pallas_call(
        kernel,
        out_shape=[jax.ShapeDtypeStruct((2, depth, width), BF16)]
        + [jax.ShapeDtypeStruct((rows, width), F32)] * 2
        + [jax.ShapeDtypeStruct(down_tile_shape(down_tile), BF16) for _ in fetch],
        in_specs=[IN_VMEM] + [IN_HBM] * 2 + [IN_PLACE] * len(after) + [IN_HBM],
        out_specs=[IN_VMEM] * (3 + len(fetch)),
        scratch_shapes=[
            pltpu.SemaphoreType.DMA((2, 2)),
            pltpu.SemaphoreType.DMA((len(fetch),)),
        ],
        compiler_params=params(8),
        cost_estimate=up_cost(1, rows, depth, width),
        name="own_block",
    )(x, gate_tile, up_tile, *after, down_tile)


def own_hidden(x, squares, tiles, gate_product, up_product, right, left):
    rows, width = gate_product.shape

    def kernel(x_ref, squares_ref, tiles_ref, gate_ref, up_ref, right_ref, left_ref, upper_ref, lower_ref, gates, ups):
        _, side, _ = position()

        @pl.when(side == 0)
        def _():
            gates[...] = gate_ref[...]
            ups[...] = up_ref[...]

        @pl.when(side == 1)
        def _():
            gates[...] = jnp.dot(x_ref[...], tiles_ref[0], preferred_element_type=F32)
            ups[...] = jnp.dot(x_ref[...], tiles_ref[1], preferred_element_type=F32)

        def total(own, start, size):
            place = slice(start, start + size)
            return own + right_ref[:, place].astype(F32) + left_ref[:, place].astype(F32)

        lanes = total(squares_ref[...], 0, LANES)
        scale = lax.rsqrt(jnp.sum(lanes, axis=1, keepdims=True) / D + 1e-05)
        gate = total(gates[...], LANES, width) * scale
        up = total(ups[...], LANES + width, width) * scale
        hidden = (gate / (1.0 + jnp.exp(-gate)) * up).astype(BF16)
        upper_ref[...] = hidden[: rows // 2]
        lower_ref[...] = hidden[rows // 2 :]

    return pl.pallas_call(
        kernel,
        out_shape=[jax.ShapeDtypeStruct((rows // 2, width), BF16)] * 2,
        in_specs=[IN_VMEM] * 7,
        out_specs=[IN_VMEM] * 2,
        scratch_shapes=[pltpu.VMEM((rows, width), F32)] * 2,
        compiler_params=params(8),
        cost_estimate=up_cost(1, rows, x.shape[1], width),
        name="own_hidden",
    )(x, squares, tiles, gate_product, up_product, right, left)


def down_tile_shape(down_tile):
    return (down_tile.shape[0] // D_WAYS, down_tile.shape[1])


def start_down_copies(place, distances, down_refs, tiles, arrived):
    copies = []
    for j, distance in enumerate(distances):
        depth = tiles[j].shape[0]
        start = pl.multiple_of(at(place, distance) * depth, LANES)
        copy = pltpu.make_async_copy(down_refs[0].at[pl.ds(start, depth), :], tiles[j], arrived.at[j])
        copy.start()
        copies.append(copy)
    return copies


def down_cost(count, rows, depth, width):
    return pl.CostEstimate(
        flops=2 * count * rows * depth * width,
        bytes_accessed=2 * count * depth * width,
        transcendentals=0,
    )


def down_blocks(total, hidden, tiles, down_tile, fetch, after):
    depth, width = tiles[0].shape
    half = hidden[0][0].shape[0]
    rows = 2 * half
    count = len(hidden)
    totals = [] if total is None else [total]
    downs = [down_tile] if fetch else []

    def kernel(*rest):
        total_refs, rest = rest[: len(totals)], rest[len(totals) :]
        hidden_refs, tile_refs, rest = rest[: 2 * count], rest[2 * count : 3 * count], rest[3 * count :]
        down_refs, rest = rest[: len(downs)], rest[len(downs) + len(after) :]
        out_ref, *fetched, whole, arrived = rest
        _, _, place = position()
        ahead = start_down_copies(place, fetch, down_refs, fetched, arrived)
        value = total_refs[0][...] if totals else jnp.zeros((rows, width), F32)
        for j, tile_ref in enumerate(tile_refs):
            whole[j, :half] = hidden_refs[2 * j][...]
            whole[j, half:] = hidden_refs[2 * j + 1][...]
            value = value + jnp.dot(whole[j], tile_ref[...], preferred_element_type=F32)
        out_ref[...] = value
        for copy in ahead:
            copy.wait()

    return pl.pallas_call(
        kernel,
        out_shape=[jax.ShapeDtypeStruct((rows, width), F32)]
        + [jax.ShapeDtypeStruct((depth, width), BF16)] * len(fetch),
        in_specs=[IN_VMEM] * (len(totals) + 3 * count) + [IN_HBM] * len(downs) + [IN_PLACE] * len(after),
        out_specs=[IN_VMEM] * (1 + len(fetch)),
        scratch_shapes=[
            pltpu.VMEM((count, rows, depth), BF16),
            pltpu.SemaphoreType.DMA((max(len(fetch), 1),)),
        ],
        compiler_params=params(8),
        cost_estimate=down_cost(count + len(fetch), rows, depth, width),
        name="down_blocks",
    )(*totals, *[half for pair in hidden for half in pair], *tiles, *downs, *after)


def last_down_block(total, upper, lower, tile):
    depth, width = tile.shape
    rows = total.shape[0]
    half = width // 2

    def kernel(total_ref, upper_ref, lower_ref, tile_ref, kept_ref, sent_ref, hidden):
        _, side, _ = position()
        hidden[: rows // 2] = upper_ref[...]
        hidden[rows // 2 :] = lower_ref[...]
        value = total_ref[...] + jnp.dot(hidden[...], tile_ref[...], preferred_element_type=F32)
        high = side == 1
        kept_ref[...] = jnp.where(high, value[:, half:], value[:, :half])
        sent_ref[...] = jnp.where(high, value[:, :half], value[:, half:]).astype(BF16)

    return pl.pallas_call(
        kernel,
        out_shape=[
            jax.ShapeDtypeStruct((rows, half), F32),
            jax.ShapeDtypeStruct((rows, half), BF16),
        ],
        in_specs=[IN_VMEM] * 4,
        out_specs=[IN_VMEM] * 2,
        scratch_shapes=[pltpu.VMEM((rows, depth), BF16)],
        compiler_params=params(8),
        cost_estimate=down_cost(1, rows, depth, width),
        name="last_down_block",
    )(total, upper, lower, tile)


def ring(stream, table_rows, token_ids, norm_gain, gate_tile, up_tile, down_tile):
    f_ways = lax.axis_size("tp") // D_WAYS
    width = gate_tile.shape[1] // D_WAYS
    rows = stream.shape[0]
    order = [0, 2, 4, 6, 7, 5, 3, 1]

    def shift(value, step):
        pairs = [
            (order[p] * f_ways + f, order[(p + step) % D_WAYS] * f_ways + f)
            for p in range(D_WAYS)
            for f in range(f_ways)
        ]
        return lax.ppermute(value, "tp", pairs)

    far_tiles = fetch_up_block(gate_tile, up_tile, 4)
    block_in, own = add_rows(token_ids, stream, table_rows, norm_gain[None], far_tiles)
    other = from_partner(own, "tp", 0)

    right, left, scaled, squares, ahead_tile = first_up_block(own, other, far_tiles, gate_tile)
    split = LANES + width
    down_tiles = []
    for distance, fetch in ((3, ()), (2, (0, -1)), (1, (1, -2))):
        ahead = ahead_tile if distance == 3 else None
        distances = [distance, -distance]
        found = up_blocks(scaled, squares, gate_tile, up_tile, distances, [right, left], down_tile, fetch, ahead)
        own = found[:2]
        down_tiles += found[2:]
        right, left = shift(right, 1), shift(left, -1)
        if distance == 3:
            right = jnp.concatenate([own[0][:, :split] + right.astype(F32), own[0][:, split:]], 1)
            left = jnp.concatenate([own[1][:, :split], own[1][:, split:] + left.astype(F32)], 1)
            right, left = right.astype(BF16), left.astype(BF16)
        else:
            right = (own[0] + right.astype(F32)).astype(BF16)
            left = (own[1] + left.astype(F32)).astype(BF16)
    own_tiles, gates, ups, *found = own_block(scaled, gate_tile, up_tile, [right, left], down_tile, (2, -3, 3, 4))
    down_tiles += found
    right, left = shift(right, 1), shift(left, -1)
    upper, lower = own_hidden(scaled, squares, own_tiles, gates, ups, right, left)

    total = None
    hidden = [(upper, lower)]
    upper_right, upper_left, lower_right, lower_left = upper, upper, lower, lower
    for distance, fetch in ((0, ()), (1, ()), (2, ()), (3, ())):
        tiles, down_tiles = down_tiles[: len(hidden)], down_tiles[len(hidden) :]
        upper_right = shift(upper_right, 1)
        lower_left = shift(lower_left, -1)
        if distance < 3:
            upper_left = shift(upper_left, -1)
            lower_right = shift(lower_right, 1)
            after = [upper_right, upper_left]
        else:
            after = []
        total, *fetched = down_blocks(total, hidden, tiles, down_tile, fetch, after)
        down_tiles += fetched
        lower_right, lower_left, total = lax.optimization_barrier((lower_right, lower_left, total))
        hidden = [(upper_right, lower_right), (upper_left, lower_left)]
    (far_tile,) = down_tiles
    kept, sent = last_down_block(total, upper_right, lower_left, far_tile)
    summed = kept + from_partner(sent, "tp", 0).astype(F32)
    return (block_in.astype(F32) + summed).astype(BF16)


def on_device(stream, table_rows, token_ids, norm_gain, gate_weight, up_weight, down_weight):
    units = gate_weight.shape[2]
    fits = lax.axis_size("tp") == 2 * D_WAYS and units % (D_WAYS * LANES) == 0
    body = ring if fits else general
    current = body(
        stream, table_rows, token_ids, norm_gain, gate_weight[0], up_weight[0], down_weight[0]
    )
    return current[None]


def solution(mesh):
    placed = (
        P("groups", "tp"),
        P("groups", "tp"),
        P(None, "groups"),
        P(),
        P("tp", None, None),
        P("tp", None, None),
        P("tp", None, None),
    )
    return jax.shard_map(
        on_device, mesh=mesh, in_specs=placed, out_specs=P(None, "groups", "tp"), check_vma=False
    )
```

```python
import jax
import jax.numpy as jnp
from jax import lax
from jax.experimental import pallas as pl
from jax.experimental.pallas import tpu as pltpu
from jax.sharding import PartitionSpec as P

D = 8192
D_WAYS = 8
LANES = 128
MIB = 2**20
BF16 = jnp.bfloat16
F32 = jnp.float32
IN_VMEM = pl.BlockSpec(memory_space=pltpu.VMEM)
IN_PLACE = pl.BlockSpec(memory_space=pl.ANY)
IN_HBM = pl.BlockSpec(memory_space=pltpu.HBM)


def from_partner(value, axis, distance):
    mask = 2**distance
    pairs = [(source, source ^ mask) for source in range(lax.axis_size(axis))]
    return lax.ppermute(value, axis, pairs)


def bit_high(index, bit):
    return index // 2**bit % 2 == 1


def gather_block(local_rows, index, low_bits):
    piece = local_rows
    for bit in range(low_bits):
        other = from_partner(piece, "tp", bit)
        piece = jnp.where(
            bit_high(index, bit),
            jnp.concatenate([other, piece], 1),
            jnp.concatenate([piece, other], 1),
        )
    return piece


def halve_columns(values, index, bit):
    width = values.shape[-1] // 2
    lower = values[..., :width]
    upper = values[..., width:]
    high = bit_high(index, bit)
    return (jnp.where(high, upper, lower), jnp.where(high, lower, upper))


def sum_blocks(partial_value, index, low_bits):
    for bit in reversed(range(low_bits)):
        kept, sent = halve_columns(partial_value, index, bit)
        partial_value = kept + from_partner(sent.astype(BF16), "tp", bit).astype(sent.dtype)
    return partial_value


def general(stream, table_rows, token_ids, norm_gain, gate_tile, up_tile, down_tile):
    f_ways = lax.axis_size("tp") // D_WAYS
    low_bits = f_ways.bit_length() - 1
    high_bits = D_WAYS.bit_length() - 1
    index = lax.axis_index("tp")
    block_pos = index // f_ways
    width = gate_tile.shape[0]
    gain_block = lax.dynamic_slice_in_dim(norm_gain, block_pos * width, width)
    picked = jnp.take(table_rows, token_ids[0], axis=0)
    block_in = (stream.astype(F32) + picked.astype(F32)).astype(BF16)
    feature_block = gather_block(block_in, index, low_bits).astype(F32)
    total = jnp.sum(feature_block * feature_block, axis=1)
    for level in range(high_bits):
        total = total + from_partner(total, "tp", low_bits + level)
    scale_rows = lax.rsqrt(total[:, None] / D + 1e-05)
    normed = (feature_block * scale_rows * gain_block[None, :]).astype(BF16)
    pair = jnp.stack(
        [
            jnp.dot(normed, gate_tile, preferred_element_type=F32),
            jnp.dot(normed, up_tile, preferred_element_type=F32),
        ],
        axis=0,
    )
    for level in range(high_bits):
        pair = pair + from_partner(pair, "tp", low_bits + level)
    hidden = (jax.nn.silu(pair[0]) * pair[1]).astype(BF16)
    partial_value = jnp.dot(hidden, down_tile, preferred_element_type=F32)
    summed = sum_blocks(partial_value, index, low_bits)
    return (block_in.astype(F32) + summed).astype(BF16)


def params(mib=26):
    return pltpu.CompilerParams(vmem_limit_bytes=mib * MIB)


def position():
    index = lax.axis_index("tp")
    block = lax.shift_right_logical(index, 1)
    half = lax.shift_right_logical(block, 1)
    place = jnp.where((block & 1) == 0, half, D_WAYS - 1 - half)
    return block, index & 1, place


def at(place, distance):
    return (place + distance + D_WAYS) & (D_WAYS - 1)


def fetch_up_block(gate_tile, up_tile, distance):
    depth, units = gate_tile.shape
    width = units // D_WAYS

    def kernel(gate_ref, up_ref, out_ref, arrived):
        _, _, place = position()
        for _, _, copy in start_up_copies(at(place, distance), gate_ref, up_ref, out_ref, arrived):
            copy.wait()

    return pl.pallas_call(
        kernel,
        out_shape=jax.ShapeDtypeStruct((2, depth, width), BF16),
        in_specs=[IN_HBM] * 2,
        out_specs=IN_VMEM,
        scratch_shapes=[pltpu.SemaphoreType.DMA((2, 1))],
        compiler_params=params(),
        name="fetch_up_block",
    )(gate_tile, up_tile)


def add_rows(token_ids, stream, table_rows, gain, after):
    entries = table_rows.shape[0]
    rows, share = stream.shape

    def kernel(ids_ref, stream_ref, table_ref, gain_ref, after_ref, out_ref, message_ref):
        place = pl.multiple_of(lax.axis_index("tp") * share, LANES)
        row = lax.broadcasted_iota(jnp.int32, (rows, rows), 0)
        column = lax.broadcasted_iota(jnp.int32, (rows, rows), 1)
        across = jnp.broadcast_to(ids_ref[...].astype(F32), (rows, rows))
        ids = jnp.sum(jnp.where(row == column, across, 0.0), axis=1, keepdims=True).astype(jnp.int32)
        entry = lax.broadcasted_iota(jnp.int32, (rows, entries), 1)
        chosen = jnp.where(entry == ids, 1.0, 0.0).astype(BF16)
        picked = jnp.dot(chosen, table_ref[...], preferred_element_type=F32)
        value = (stream_ref[...].astype(F32) + picked).astype(BF16)
        out_ref[...] = value
        value = value.astype(F32)
        squares = jnp.zeros((rows, LANES), F32)
        for lane in range(0, share, LANES):
            squares += value[:, lane : lane + LANES] * value[:, lane : lane + LANES]
        message_ref[:, share:] = squares.astype(BF16)
        message_ref[:, :share] = (value * gain_ref[:, pl.ds(place, share)]).astype(BF16)

    return pl.pallas_call(
        kernel,
        out_shape=[
            jax.ShapeDtypeStruct((rows, share), BF16),
            jax.ShapeDtypeStruct((rows, share + LANES), BF16),
        ],
        in_specs=[IN_VMEM] * 4 + [IN_PLACE],
        out_specs=[IN_VMEM] * 2,
        compiler_params=params(),
        name="add_rows",
    )(token_ids, stream, table_rows, gain, after)


def start_up_copies(block, gate_ref, up_ref, tiles, arrived, skipped=None, skip=None):
    cuts = arrived.shape[1]
    cut = gate_ref.shape[0] // cuts
    width = gate_ref.shape[1] // D_WAYS
    columns = pl.ds(pl.multiple_of(block * width, LANES), width)
    copies = []
    for m, ref in enumerate((gate_ref, up_ref)):
        for c in range(cuts):
            features = slice(c * cut, (c + 1) * cut)
            copy = pltpu.make_async_copy(
                ref.at[pl.ds(c * cut, cut), columns], tiles.at[m, pl.ds(c * cut, cut), :], arrived.at[m, c]
            )
            if m == skipped:
                pl.when(jnp.logical_not(skip))(copy.start)
            else:
                copy.start()
            copies.append((m, features, copy))
    return copies


def up_products(x_ref, copies, tiles, out_refs):
    for m, features, copy in copies:
        copy.wait()
        product = jnp.dot(x_ref[:, features], tiles[m, features, :], preferred_element_type=F32)
        if features.start == 0:
            out_refs[m][...] = product
        else:
            out_refs[m][...] += product


def up_products_ahead(x_ref, copies, tiles, out_refs, gate_here, ahead_ref):
    @pl.when(gate_here)
    def _():
        out_refs[0][...] = jnp.dot(x_ref[...], ahead_ref[...], preferred_element_type=F32)

    @pl.when(jnp.logical_not(gate_here))
    def _():
        up_products(x_ref, [copy for copy in copies if copy[0] == 0], tiles, out_refs)

    up_products(x_ref, [copy for copy in copies if copy[0] == 1], tiles, out_refs)


def up_scratch(count, depth, width):
    cuts = 2
    return [
        pltpu.VMEM((count, 2, depth, width), BF16),
        pltpu.SemaphoreType.DMA((count, 2, cuts)),
    ]


def up_cost(count, rows, depth, width):
    return pl.CostEstimate(
        flops=4 * count * rows * depth * width,
        bytes_accessed=4 * count * depth * width,
        transcendentals=0,
    )


def first_up_block(own, other, tiles, gate_tile):
    _, depth, width = tiles.shape
    rows = own.shape[0]
    share = own.shape[1] - LANES

    def kernel(own_ref, other_ref, tiles_ref, gate_ref, gate_out, up_out, x_ref, squares_ref, ahead_ref, arrived):
        _, side, place = position()
        high = side == 1
        columns = pl.ds(pl.multiple_of(at(place, 3) * width, LANES), width)
        copy = pltpu.make_async_copy(gate_ref.at[:, columns], ahead_ref, arrived)

        @pl.when(side == 0)
        def _():
            copy.start()

        own_x, other_x = own_ref[:, :share], other_ref[:, :share]
        x_ref[:, :share] = jnp.where(high, other_x, own_x)
        x_ref[:, share:] = jnp.where(high, own_x, other_x)
        squares = own_ref[:, share:].astype(F32) + other_ref[:, share:].astype(F32)
        squares_ref[...] = squares
        gate_out[:, :LANES] = squares.astype(BF16)
        x = x_ref[...]
        gate_out[:, LANES:] = jnp.dot(x, tiles_ref[0], preferred_element_type=F32).astype(BF16)
        up_out[...] = jnp.dot(x, tiles_ref[1], preferred_element_type=F32).astype(BF16)

        @pl.when(side == 0)
        def _():
            copy.wait()

    return pl.pallas_call(
        kernel,
        out_shape=[
            jax.ShapeDtypeStruct((rows, LANES + width), BF16),
            jax.ShapeDtypeStruct((rows, width), BF16),
            jax.ShapeDtypeStruct((rows, depth), BF16),
            jax.ShapeDtypeStruct((rows, LANES), F32),
            jax.ShapeDtypeStruct((depth, width), BF16),
        ],
        in_specs=[IN_VMEM] * 3 + [IN_HBM],
        out_specs=[IN_VMEM] * 5,
        scratch_shapes=[pltpu.SemaphoreType.DMA],
        compiler_params=params(),
        cost_estimate=up_cost(1, rows, depth, width),
        name="first_up_block",
    )(own, other, tiles, gate_tile)


def up_blocks(x, squares, gate_tile, up_tile, distances, after, down_tile=None, fetch=(), ahead_tile=None):
    depth, units = gate_tile.shape
    width = units // D_WAYS
    rows = x.shape[0]
    count = len(distances)
    downs = [down_tile] if fetch else []
    aheads = [] if ahead_tile is None else [ahead_tile]

    def kernel(x_ref, squares_ref, gate_ref, up_ref, *rest):
        rest = rest[len(after) :]
        down_refs, rest = rest[: len(downs)], rest[len(downs) :]
        ahead_refs, rest = rest[: len(aheads)], rest[len(aheads) :]
        out_refs, fetched = rest[:count], rest[count : count + len(fetch)]
        tiles, arrived, fetch_arrived = rest[-3:]
        _, side, place = position()
        here = side == 0
        copies = [
            start_up_copies(
                at(place, distance),
                gate_ref,
                up_ref,
                tiles.at[j],
                arrived.at[j],
                0 if j == 0 and aheads else None,
                here,
            )
            for j, distance in enumerate(distances)
        ]
        ahead = start_down_copies(place, fetch, down_refs, fetched, fetch_arrived)
        for j, out_ref in enumerate(out_refs):
            out_ref[:, :LANES] = squares_ref[...]
            pair = [out_ref.at[:, pl.ds(LANES, width)], out_ref.at[:, pl.ds(LANES + width, width)]]
            if j == 0 and aheads:
                up_products_ahead(x_ref, copies[j], tiles.at[j], pair, here, ahead_refs[0])
            else:
                up_products(x_ref, copies[j], tiles.at[j], pair)
        for copy in ahead:
            copy.wait()

    return pl.pallas_call(
        kernel,
        out_shape=[jax.ShapeDtypeStruct((rows, LANES + 2 * width), F32)] * count
        + [jax.ShapeDtypeStruct(down_tile_shape(down_tile), BF16) for _ in fetch],
        in_specs=[IN_VMEM] * 2
        + [IN_HBM] * 2
        + [IN_PLACE] * len(after)
        + [IN_HBM] * len(downs)
        + [IN_VMEM] * len(aheads),
        out_specs=[IN_VMEM] * (count + len(fetch)),
        scratch_shapes=up_scratch(count, depth, width) + [pltpu.SemaphoreType.DMA((max(len(fetch), 1),))],
        compiler_params=params(26 if count == 2 else 14),
        cost_estimate=up_cost(count, rows, depth, width),
        name="up_blocks",
    )(x, squares, gate_tile, up_tile, *after, *downs, *aheads)


def own_block(x, gate_tile, up_tile, after, down_tile, fetch):
    depth, units = gate_tile.shape
    width = units // D_WAYS
    rows = x.shape[0]

    def kernel(x_ref, gate_ref, up_ref, *rest):
        down_ref, tiles, gate_out, up_out, *fetched, arrived, fetch_arrived = rest[len(after) :]
        _, side, place = position()
        copies = start_up_copies(at(place, 0), gate_ref, up_ref, tiles, arrived)
        ahead = start_down_copies(place, fetch, [down_ref], fetched, fetch_arrived)

        @pl.when(side == 0)
        def _():
            up_products(x_ref, copies, tiles, [gate_out, up_out])

        @pl.when(side == 1)
        def _():
            for _, _, copy in copies:
                copy.wait()

        for copy in ahead:
            copy.wait()

    return pl.pallas_call(
        kernel,
        out_shape=[jax.ShapeDtypeStruct((2, depth, width), BF16)]
        + [jax.ShapeDtypeStruct((rows, width), F32)] * 2
        + [jax.ShapeDtypeStruct(down_tile_shape(down_tile), BF16) for _ in fetch],
        in_specs=[IN_VMEM] + [IN_HBM] * 2 + [IN_PLACE] * len(after) + [IN_HBM],
        out_specs=[IN_VMEM] * (3 + len(fetch)),
        scratch_shapes=[
            pltpu.SemaphoreType.DMA((2, 2)),
            pltpu.SemaphoreType.DMA((len(fetch),)),
        ],
        compiler_params=params(8),
        cost_estimate=up_cost(1, rows, depth, width),
        name="own_block",
    )(x, gate_tile, up_tile, *after, down_tile)


def own_hidden(x, squares, tiles, gate_product, up_product, right, left):
    rows, width = gate_product.shape

    def kernel(x_ref, squares_ref, tiles_ref, gate_ref, up_ref, right_ref, left_ref, upper_ref, lower_ref, gates, ups):
        _, side, _ = position()

        @pl.when(side == 0)
        def _():
            gates[...] = gate_ref[...]
            ups[...] = up_ref[...]

        @pl.when(side == 1)
        def _():
            gates[...] = jnp.dot(x_ref[...], tiles_ref[0], preferred_element_type=F32)
            ups[...] = jnp.dot(x_ref[...], tiles_ref[1], preferred_element_type=F32)

        def total(own, start, size):
            place = slice(start, start + size)
            return own + right_ref[:, place].astype(F32) + left_ref[:, place].astype(F32)

        lanes = total(squares_ref[...], 0, LANES)
        scale = lax.rsqrt(jnp.sum(lanes, axis=1, keepdims=True) / D + 1e-05)
        gate = total(gates[...], LANES, width) * scale
        up = total(ups[...], LANES + width, width) * scale
        hidden = (gate / (1.0 + jnp.exp(-gate)) * up).astype(BF16)
        upper_ref[...] = hidden[: rows // 2]
        lower_ref[...] = hidden[rows // 2 :]

    return pl.pallas_call(
        kernel,
        out_shape=[jax.ShapeDtypeStruct((rows // 2, width), BF16)] * 2,
        in_specs=[IN_VMEM] * 7,
        out_specs=[IN_VMEM] * 2,
        scratch_shapes=[pltpu.VMEM((rows, width), F32)] * 2,
        compiler_params=params(8),
        cost_estimate=up_cost(1, rows, x.shape[1], width),
        name="own_hidden",
    )(x, squares, tiles, gate_product, up_product, right, left)


def down_tile_shape(down_tile):
    return (down_tile.shape[0] // D_WAYS, down_tile.shape[1])


def start_down_copies(place, distances, down_refs, tiles, arrived):
    copies = []
    for j, distance in enumerate(distances):
        depth = tiles[j].shape[0]
        start = pl.multiple_of(at(place, distance) * depth, LANES)
        copy = pltpu.make_async_copy(down_refs[0].at[pl.ds(start, depth), :], tiles[j], arrived.at[j])
        copy.start()
        copies.append(copy)
    return copies


def down_cost(count, rows, depth, width):
    return pl.CostEstimate(
        flops=2 * count * rows * depth * width,
        bytes_accessed=2 * count * depth * width,
        transcendentals=0,
    )


def down_blocks(total, hidden, tiles, down_tile, fetch, after):
    depth, width = tiles[0].shape
    half = hidden[0][0].shape[0]
    rows = 2 * half
    count = len(hidden)
    totals = [] if total is None else [total]
    downs = [down_tile] if fetch else []

    def kernel(*rest):
        total_refs, rest = rest[: len(totals)], rest[len(totals) :]
        hidden_refs, tile_refs, rest = rest[: 2 * count], rest[2 * count : 3 * count], rest[3 * count :]
        down_refs, rest = rest[: len(downs)], rest[len(downs) + len(after) :]
        out_ref, *fetched, whole, arrived = rest
        _, _, place = position()
        ahead = start_down_copies(place, fetch, down_refs, fetched, arrived)
        value = total_refs[0][...] if totals else jnp.zeros((rows, width), F32)
        for j, tile_ref in enumerate(tile_refs):
            whole[j, :half] = hidden_refs[2 * j][...]
            whole[j, half:] = hidden_refs[2 * j + 1][...]
            value = value + jnp.dot(whole[j], tile_ref[...], preferred_element_type=F32)
        out_ref[...] = value
        for copy in ahead:
            copy.wait()

    return pl.pallas_call(
        kernel,
        out_shape=[jax.ShapeDtypeStruct((rows, width), F32)]
        + [jax.ShapeDtypeStruct((depth, width), BF16)] * len(fetch),
        in_specs=[IN_VMEM] * (len(totals) + 3 * count) + [IN_HBM] * len(downs) + [IN_PLACE] * len(after),
        out_specs=[IN_VMEM] * (1 + len(fetch)),
        scratch_shapes=[
            pltpu.VMEM((count, rows, depth), BF16),
            pltpu.SemaphoreType.DMA((max(len(fetch), 1),)),
        ],
        compiler_params=params(8),
        cost_estimate=down_cost(count + len(fetch), rows, depth, width),
        name="down_blocks",
    )(*totals, *[half for pair in hidden for half in pair], *tiles, *downs, *after)


def last_down_block(total, upper, lower, tile):
    depth, width = tile.shape
    rows = total.shape[0]
    half = width // 2

    def kernel(total_ref, upper_ref, lower_ref, tile_ref, kept_ref, sent_ref, hidden):
        _, side, _ = position()
        hidden[: rows // 2] = upper_ref[...]
        hidden[rows // 2 :] = lower_ref[...]
        value = total_ref[...] + jnp.dot(hidden[...], tile_ref[...], preferred_element_type=F32)
        high = side == 1
        kept_ref[...] = jnp.where(high, value[:, half:], value[:, :half])
        sent_ref[...] = jnp.where(high, value[:, :half], value[:, half:]).astype(BF16)

    return pl.pallas_call(
        kernel,
        out_shape=[
            jax.ShapeDtypeStruct((rows, half), F32),
            jax.ShapeDtypeStruct((rows, half), BF16),
        ],
        in_specs=[IN_VMEM] * 4,
        out_specs=[IN_VMEM] * 2,
        scratch_shapes=[pltpu.VMEM((rows, depth), BF16)],
        compiler_params=params(8),
        cost_estimate=down_cost(1, rows, depth, width),
        name="last_down_block",
    )(total, upper, lower, tile)


def ring(stream, table_rows, token_ids, norm_gain, gate_tile, up_tile, down_tile):
    f_ways = lax.axis_size("tp") // D_WAYS
    width = gate_tile.shape[1] // D_WAYS
    rows = stream.shape[0]
    order = [0, 2, 4, 6, 7, 5, 3, 1]

    def shift(value, step):
        pairs = [
            (order[p] * f_ways + f, order[(p + step) % D_WAYS] * f_ways + f)
            for p in range(D_WAYS)
            for f in range(f_ways)
        ]
        return lax.ppermute(value, "tp", pairs)

    far_tiles = fetch_up_block(gate_tile, up_tile, 4)
    block_in, own = add_rows(token_ids, stream, table_rows, norm_gain[None], far_tiles)
    other = from_partner(own, "tp", 0)

    right, left, scaled, squares, ahead_tile = first_up_block(own, other, far_tiles, gate_tile)
    split = LANES + width
    down_tiles = []
    for distance, fetch in ((3, ()), (2, (0, -1)), (1, (1, -2))):
        ahead = ahead_tile if distance == 3 else None
        distances = [distance, -distance]
        found = up_blocks(scaled, squares, gate_tile, up_tile, distances, [right, left], down_tile, fetch, ahead)
        own = found[:2]
        down_tiles += found[2:]
        right, left = shift(right, 1), shift(left, -1)
        if distance == 3:
            right = jnp.concatenate([own[0][:, :split] + right.astype(F32), own[0][:, split:]], 1)
            left = jnp.concatenate([own[1][:, :split], own[1][:, split:] + left.astype(F32)], 1)
            right, left = right.astype(BF16), left.astype(BF16)
        else:
            right = (own[0] + right.astype(F32)).astype(BF16)
            left = (own[1] + left.astype(F32)).astype(BF16)
    own_tiles, gates, ups, *found = own_block(scaled, gate_tile, up_tile, [right, left], down_tile, (2, -3, 3, 4))
    down_tiles += found
    right, left = shift(right, 1), shift(left, -1)
    upper, lower = own_hidden(scaled, squares, own_tiles, gates, ups, right, left)

    total = None
    hidden = [(upper, lower)]
    upper_right, upper_left, lower_right, lower_left = upper, upper, lower, lower
    for distance, fetch in ((0, ()), (1, ()), (2, ()), (3, ())):
        tiles, down_tiles = down_tiles[: len(hidden)], down_tiles[len(hidden) :]
        upper_right = shift(upper_right, 1)
        lower_left = shift(lower_left, -1)
        if distance < 3:
            upper_left = shift(upper_left, -1)
            lower_right = shift(lower_right, 1)
            after = [upper_right, lower_left]
        else:
            after = []
        total, *fetched = down_blocks(total, hidden, tiles, down_tile, fetch, after)
        down_tiles += fetched
        upper_left, lower_right, total = lax.optimization_barrier((upper_left, lower_right, total))
        hidden = [(upper_right, lower_right), (upper_left, lower_left)]
    (far_tile,) = down_tiles
    kept, sent = last_down_block(total, upper_right, lower_left, far_tile)
    summed = kept + from_partner(sent, "tp", 0).astype(F32)
    return (block_in.astype(F32) + summed).astype(BF16)


def on_device(stream, table_rows, token_ids, norm_gain, gate_weight, up_weight, down_weight):
    units = gate_weight.shape[2]
    fits = lax.axis_size("tp") == 2 * D_WAYS and units % (D_WAYS * LANES) == 0
    body = ring if fits else general
    current = body(
        stream, table_rows, token_ids, norm_gain, gate_weight[0], up_weight[0], down_weight[0]
    )
    return current[None]


def solution(mesh):
    placed = (
        P("groups", "tp"),
        P("groups", "tp"),
        P(None, "groups"),
        P(),
        P("tp", None, None),
        P("tp", None, None),
        P("tp", None, None),
    )
    return jax.shard_map(
        on_device, mesh=mesh, in_specs=placed, out_specs=P(None, "groups", "tp"), check_vma=False
    )
```
